32 devices in a mesh: grp: 2 (over x), chan: 16 (over z, y, core).
Axes of the slice: x: 2, y: 2, z: 4, core: 2. Of those that a mesh axis runs over, the one named last changes fastest.
Arguments:
- traces: bfloat16 [32, 16, 256, 512], P(('grp', 'chan')), parts along dimension 0, may hold values from -6 to 6
- mask: int32 [32, 16], P('grp'), parts along dimension 0, may hold values 0 or 1
- counts: int32 [32], P('grp'), parts along dimension 0, may hold values from 0 to 5, as said below
Outputs:
- forward: float32 [32, 5, 128, 512], P(('grp', 'chan')), parts along dimension 0
- backward: float32 [32, 5, 128, 512], P(('grp', 'chan')), parts along dimension 0
The draws below stay inside these ranges and needn't reach their ends.
There are 2 independent parts, one for each index of `grp`. The reference program is written for one: setup_inputs(seed, part) draws one part's arguments, and reference() takes and returns one part's arrays. A program takes and returns all parts, laid end to end along the dimension named above; each array names one. Nothing has to cross between parts.
Inputs may be any that keep to these rules, and one draw needn't show every extreme that they name: counts[b] <= min(5, 15 - b); block 0 always has 5 partners.
All inputs are finite; a program needn't handle non-finite values.
Results may differ from the reference program's by a relative error of at most 0.0063.
Values may be sent and summed in bfloat16 or wider, within the bound.
No kernel may reach another device: no remote copies, remote signals or barrier semaphores. Data moves between devices by JAX's collectives and lax.ppermute only.
A program may use at most 128 MiB of HBM per device.

```python
import math
import jax
import jax.numpy as jnp
from jax import lax

CH = 512
L = 256
W = 16
MAXP = 5
BLOCKS = 16


def draw_counts(key, part):
    blocks = jnp.arange(BLOCKS, dtype=jnp.int32)
    drawn = jax.random.randint(key, (BLOCKS,), 1, MAXP + 1).astype(jnp.int32)
    drawn = jnp.where(blocks == 0, MAXP, drawn)
    return jnp.minimum(drawn, BLOCKS - 1 - blocks).astype(jnp.int32)


def with_ends(entries, stream_key, smallest, high):
    spot = [jax.random.randint(jax.random.fold_in(stream_key, axis), (), 0, length) for axis, length in enumerate(entries.shape)]
    widest = entries.shape.index(max(entries.shape))
    neighbour = spot[:widest] + [(spot[widest] + 1) % entries.shape[widest]] + spot[widest + 1:]
    return entries.at[tuple(spot)].set(smallest).at[tuple(neighbour)].set(high)


def levels(key, extent, shards, low, top_value):
    def one(axis_at, blocks):
        heights = jax.random.uniform(jax.random.fold_in(jax.random.fold_in(key, 6), axis_at), (blocks,), jnp.float32, low / len(shards), top_value / len(shards))
        return jnp.repeat(jnp.exp(heights), extent[axis_at] // blocks).reshape((-1,) + (1,) * (len(extent) - axis_at - 1))

    loudness = one(*shards[0])
    for cut in shards[1:]:
        loudness = loudness * one(*cut)
    return loudness


def noise(key, dims, scale, limit, split=(), kind=jnp.bfloat16):
    factor_of = levels(key, dims, split, -0.22, 0.18) if split else 1.0
    values = jax.random.normal(key, dims, jnp.float32) * scale * factor_of
    return jnp.minimum(jnp.maximum(values, -limit), limit).astype(kind)


def setup_inputs(seed: int = 0, part: int = 0) -> dict:
    keys = jax.random.split(jax.random.key(seed), 4)
    part_keys = jax.random.split(jax.random.fold_in(keys[3], part), 4)
    traces = noise(part_keys[0], (BLOCKS, W, L, CH), 1.0, 6.0, ((0, 16),))
    mask = with_ends((jax.random.randint(part_keys[1], (BLOCKS, W), 0, 4) < 3).astype(jnp.int32), jax.random.fold_in(part_keys[1], 1), 0, 1)
    counts = draw_counts(jax.random.fold_in(jax.random.fold_in(keys[3], part), 71), part)
    return dict(traces=traces, mask=mask, counts=counts)


def lag_table(lags, bins):
    times = jnp.arange(lags, dtype=jnp.int32)[:, None]
    freqs = jnp.arange(1, bins + 1, dtype=jnp.int32)[None, :]
    phase = (times * freqs % lags).astype(jnp.float32) * (2.0 * math.pi / lags)
    return jnp.concatenate([jnp.cos(phase), -jnp.sin(phase)], axis=1).astype(jnp.bfloat16)

def whiten(record, table):
    bins = table.shape[1] // 2
    raw = jnp.einsum('tk,wtc->wkc', table.astype(jnp.float32), record.astype(jnp.float32), precision=lax.Precision.HIGHEST)
    power = lax.optimization_barrier(jnp.sum(raw * raw, axis=1)) / bins
    return (raw / jnp.sqrt(power + 1e-06)[:, None, :]).astype(jnp.bfloat16)

def stack_pair(first, second, weight):
    half = first.shape[1] // 2
    wlen = first.shape[0]
    first_re = first[:, :half].astype(jnp.float32)
    first_im = first[:, half:].astype(jnp.float32)
    second_re = second[:, :half].astype(jnp.float32)
    second_im = second[:, half:].astype(jnp.float32)
    scaled = weight[:, None, None]
    real_part = lax.optimization_barrier(jnp.sum(scaled * (first_re * second_re + first_im * second_im), axis=0))
    imag_part = lax.optimization_barrier(jnp.sum(scaled * (first_im * second_re - first_re * second_im), axis=0))
    return (jnp.concatenate([real_part, imag_part], axis=0) / math.sqrt(wlen)).astype(jnp.bfloat16)

def pair_lags(first, second, weight, table, bins):
    stacked = stack_pair(first, second, weight)
    return jnp.dot(table, stacked, preferred_element_type=jnp.float32) / math.sqrt(bins)

def reference(traces, mask, counts):
    blocks = traces.shape[0]
    lags = traces.shape[2]
    bins = lags // 2
    table = lag_table(lags, bins)
    white = lax.map(lambda record: whiten(record, table), traces)
    valid = mask.astype(jnp.float32)

    def one_block(block):
        causal = []
        acausal = []
        for step in range(1, MAXP + 1):
            other = jnp.minimum(block + step, blocks - 1).astype(jnp.int32)
            weight = valid[block] * valid[other]
            corr = pair_lags(white[block], white[other], weight, table, bins)
            corr = jnp.where(counts[block] >= step, corr, jnp.zeros_like(corr))
            causal.append(corr[:bins])
            acausal.append(corr[bins:][::-1])
        return (jnp.stack(causal), jnp.stack(acausal))
    forward, acausal_all = lax.map(one_block, jnp.arange(blocks, dtype=jnp.int32))
    rows = jnp.arange(blocks, dtype=jnp.int32)
    backward_list = []
    for step in range(1, MAXP + 1):
        rolled = jnp.roll(acausal_all[:, step - 1], step, axis=0)
        backward_list.append(jnp.where((rows >= step)[:, None, None], rolled, jnp.zeros_like(rolled)))
    backward = jnp.stack(backward_list, axis=1)
    return (forward, backward)
```

```python
import functools
import math

import jax
import jax.numpy as jnp
import numpy as np
from jax import lax
from jax.experimental import pallas as pl
from jax.experimental.pallas import tpu as pltpu
from jax.sharding import PartitionSpec as P

MAXP = 5
PLANE = 4
HALVES = 7
VMEM = 56 * 1024 * 1024

FIRST = -3
SPOTS = 9
GROUPS = (
    ((0, 4), (0, 5), (1, 4), (1, 5), (2, 5)),
    ((0, 1), (0, 2), (0, 3), (1, 2), (1, 3), (2, 3)),
    ((-1, 0), (-1, 1), (-1, 2), (-1, 3), (-1, 4)),
    ((-2, 0), (-2, 2), (-2, 3), (-3, 2)),
)
PAIRS = tuple(pair for group in GROUPS for pair in group)


def kept(spot):
    ahead = sorted(("ahead", b - a - 1) for a, b in PAIRS if a == spot)
    back = sorted(("back", b - a - 1) for a, b in PAIRS if b == spot)
    return ahead + back


def lag_tables(lags):
    bins = lags // 2
    phase = (np.arange(lags)[:, None] * np.arange(1, bins + 1)[None, :] % lags) * (2.0 * math.pi / lags)
    real, imag = np.cos(phase), -np.sin(phase)
    causal = np.concatenate([real, imag], axis=1)
    other = np.concatenate([real, -imag], axis=1)
    near = np.concatenate([causal[:bins], causal[bins:][::-1]], axis=0)
    far = np.concatenate([other[bins:][::-1], other[:bins]], axis=0)
    return causal.astype(jnp.bfloat16), np.stack([near, far]).astype(jnp.bfloat16)


def whiten_body(where_ref, mask_ref, table_ref, traces_ref, out_ref, *, first):
    bins = table_ref.shape[0] // 2
    step = traces_ref.shape[0]
    for w in range(step):
        raw = jnp.dot(table_ref[...], traces_ref[w], preferred_element_type=jnp.float32)
        power = jnp.sum(raw * raw, axis=0, keepdims=True) / bins
        valid = mask_ref[first + pl.program_id(0) * step + w].astype(jnp.float32)
        out_ref[w] = (raw * (valid * lax.rsqrt(power + 1e-06))).astype(jnp.bfloat16)


def whiten(record, table, mask, quarter, first, count):
    windows, lags, width = record.shape
    part = width // PLANE
    step = 4
    return pl.pallas_call(
        functools.partial(whiten_body, first=first),
        grid_spec=pltpu.PrefetchScalarGridSpec(
            num_scalar_prefetch=2,
            grid=(count // step,),
            in_specs=[
                pl.BlockSpec((lags, lags), lambda i, where, mask: (0, 0)),
                pl.BlockSpec((step, lags, part), lambda i, where, mask: (first // step + i, 0, where[0])),
            ],
            out_specs=pl.BlockSpec((step, lags, part), lambda i, where, mask: (i, 0, 0)),
        ),
        out_shape=jax.ShapeDtypeStruct((count, lags, part), jnp.bfloat16),
        cost_estimate=pl.CostEstimate(flops=2 * count * lags * lags * part, bytes_accessed=4 * count * lags * part, transcendentals=0),
    )(quarter[None], mask, table, record)


def correlate_body(place_ref, counts_ref, table_ref, own, sib, o0a, o0b, o1a, o1b, x0, x1, v0a, v0b, v1a, v1b, ea, eb,
                   g0, g1, g2, g3, s0, s1, d0, d1, extra, spots, stack, gs, xs, vs, es, sems):
    windows = own.shape[0]
    half = windows // 2
    bins = own.shape[1] // 2
    part = own.shape[2]
    far, m, base = place_ref[0], place_ref[1], place_ref[2]
    blocks = counts_ref.shape[0]
    lo, hi = pl.ds(0, half), pl.ds(half, half)
    every = pl.ds(0, windows)
    moves = (
        (own, 3 + m, every), (sib, 4 - m, every), (x0, 7 + m, every), (x1, 8 - m, every),
        (o0a, 5 + m, lo), (o0b, 5 + m, hi), (o1a, 6 - m, lo), (o1b, 6 - m, hi),
        (v0a, 1 + m, lo), (v0b, 1 + m, hi), (v1a, 2 - m, lo), (v1b, 2 - m, hi),
    )
    copies = [pltpu.make_async_copy(ref, spots.at[slot, span], sems.at[i]) for i, (ref, slot, span) in enumerate(moves)]
    for copy in copies:
        copy.start()
    far_copies = [pltpu.make_async_copy(ref, spots.at[0], sems.at[len(moves)]) for ref in (ea, eb)]

    @pl.when(m == 1)
    def _():
        far_copies[0].start()

    @pl.when(m == 0)
    def _():
        far_copies[1].start()

    for copy in copies:
        copy.wait()
    far_copies[0].wait()

    rows = 16
    at = 0
    for group in GROUPS:
        need = sorted({spot for pair in group for spot in pair})

        def tile(kt, carry, group=group, need=need, at=at):
            re_rows = pl.ds(pl.multiple_of(kt * rows, rows), rows)
            im_rows = pl.ds(pl.multiple_of(bins + kt * rows, rows), rows)

            def window(w, sums):
                real = {s: spots[s - FIRST, w, re_rows, :].astype(jnp.float32) for s in need}
                imag = {s: spots[s - FIRST, w, im_rows, :].astype(jnp.float32) for s in need}
                out = []
                for n, (a, b) in enumerate(group):
                    out.append(sums[2 * n] + (real[a] * real[b] + imag[a] * imag[b]))
                    out.append(sums[2 * n + 1] + (imag[a] * real[b] - real[a] * imag[b]))
                return tuple(out)

            zero = jnp.zeros((rows, part), jnp.float32)
            sums = lax.fori_loop(0, windows, window, (zero,) * (2 * len(group)), unroll=2)
            scale = 1.0 / math.sqrt(windows)
            for n in range(len(group)):
                lanes = pl.ds((at + n) * part, part)
                stack[re_rows, lanes] = (sums[2 * n] * scale).astype(jnp.bfloat16)
                stack[im_rows, lanes] = (sums[2 * n + 1] * scale).astype(jnp.bfloat16)
            return carry

        lax.fori_loop(0, bins // rows, tile, 0)
        at += len(group)

    norm = 1.0 / math.sqrt(bins)
    for n, (a, b) in enumerate(PAIRS):
        corr = jnp.dot(table_ref[far], stack[:, n * part:(n + 1) * part], preferred_element_type=jnp.float32)
        first = jnp.where(far == 0, base + a, base + 3 - b)
        count = counts_ref[jnp.clip(first, 0, blocks - 1)]
        corr = corr * jnp.where(count >= b - a, norm, 0.0)
        ahead, back = corr[:bins].astype(jnp.bfloat16), corr[bins:].astype(jnp.bfloat16)
        if a >= 0:
            gs[a, kept(a).index(("ahead", b - a - 1))] = ahead
        elif a == -3:
            es[0] = ahead
        else:
            vs[a + 2, [d for c, d in PAIRS if c == a].index(b)] = ahead
        if b < PLANE:
            gs[b, kept(b).index(("back", b - a - 1))] = back
        else:
            xs[b - PLANE, b - a - 3] = back

    outs = ((gs.at[m], g0), (gs.at[1 - m], g1), (gs.at[2 + m], g2), (gs.at[3 - m], g3),
            (xs.at[m], s0), (xs.at[1 - m], s1), (vs.at[m], d0), (vs.at[1 - m], d1), (es, extra))
    copies = [pltpu.make_async_copy(src, dst, sems.at[i]) for i, (src, dst) in enumerate(outs)]
    for copy in copies:
        copy.start()
    for copy in copies:
        copy.wait()


def correlate(place, counts, tables, whites):
    windows, lags, part = whites[0].shape
    bins = lags // 2
    anywhere = pl.BlockSpec(memory_space=pl.ANY)
    scalars = pl.BlockSpec(memory_space=pltpu.SMEM)
    sizes = [HALVES] * 4 + [3, 3, 5, 5, 1]
    return pl.pallas_call(
        correlate_body,
        in_specs=[scalars, scalars, pl.BlockSpec(memory_space=pltpu.VMEM)] + [anywhere] * len(whites),
        out_specs=[anywhere] * len(sizes),
        out_shape=[jax.ShapeDtypeStruct((n, bins, part), jnp.bfloat16) for n in sizes],
        scratch_shapes=[
            pltpu.VMEM((SPOTS, windows, lags, part), jnp.bfloat16),
            pltpu.VMEM((lags, len(PAIRS) * part), jnp.bfloat16),
            pltpu.VMEM((PLANE, HALVES, bins, part), jnp.bfloat16),
            pltpu.VMEM((2, 3, bins, part), jnp.bfloat16),
            pltpu.VMEM((2, 5, bins, part), jnp.bfloat16),
            pltpu.VMEM((1, bins, part), jnp.bfloat16),
            pltpu.SemaphoreType.DMA((13,)),
        ],
        compiler_params=pltpu.CompilerParams(vmem_limit_bytes=VMEM),
        cost_estimate=pl.CostEstimate(flops=16 * 20 * windows * bins * part, bytes_accessed=2 * 9 * windows * lags * part, transcendentals=0),
    )(place, counts, tables, *whites)


def assemble_body(place_ref, g0, g1, g2, g3, s0, s1, d0, d1, w0, w1, forward, backward, out, sems):
    far, m, q = place_ref[0], place_ref[1], place_ref[3]
    part = g0.shape[2]

    def put(side, j, quarter, value):
        lanes = pl.ds(pl.multiple_of(quarter * part, part), part)
        out[side, j, :, lanes] = value.astype(jnp.float32)

    def fill(spot, k, near, distant, last):
        quarter = q ^ k
        ahead = far if k < 2 else 1 - far
        have = kept(spot)
        for n, (kind, j) in enumerate(have):
            put(ahead if kind == "ahead" else 1 - ahead, j, quarter, near[n])
        if spot < 2:
            for n in range(3):
                put(1 - ahead, 2 + n, quarter, distant[n])
            if spot == 1:
                put(ahead, 4, quarter, last[0])
        else:
            missing = [j for j in range(MAXP) if ("ahead", j) not in have]
            for n, j in enumerate(missing):
                put(ahead, j, quarter, distant[n])

    for mine in range(2):
        @pl.when(m == mine)
        def _(mine=mine):
            fill(mine, 0, g0, s0, w0)
            fill(mine, 1, g1, s1, w1)
            fill(3 - mine, 2, g2, d0, None)
            fill(3 - mine, 3, g3, d1, None)

    copies = [pltpu.make_async_copy(out.at[side], ref.at[0], sems.at[side]) for side, ref in enumerate((forward, backward))]
    for copy in copies:
        copy.start()
    for copy in copies:
        copy.wait()


def assemble(place, parts, shape):
    scalars = pl.BlockSpec(memory_space=pltpu.SMEM)
    return pl.pallas_call(
        assemble_body,
        in_specs=[scalars] + [pl.BlockSpec(memory_space=pltpu.VMEM)] * len(parts),
        out_specs=[pl.BlockSpec(memory_space=pl.ANY)] * 2,
        out_shape=[jax.ShapeDtypeStruct((1,) + shape, jnp.float32)] * 2,
        scratch_shapes=[pltpu.VMEM((2,) + shape, jnp.float32), pltpu.SemaphoreType.DMA((2,))],
        compiler_params=pltpu.CompilerParams(vmem_limit_bytes=VMEM),
    )(place, *parts)


def local(traces, mask, counts):
    peers = lax.axis_size("chan")
    record = traces[0]
    windows, lags, width = record.shape
    me = lax.axis_index("chan").astype(jnp.int32)
    q = me % PLANE
    far = q // 2
    m = (q % 2) ^ far
    place = jnp.stack([far, m, me - q, q])
    own_mask = lax.dynamic_index_in_dim(mask, me, 0, keepdims=False)
    causal, tables = lag_tables(lags)
    rows = jnp.asarray(np.ascontiguousarray(causal.T))

    def send(value, flip, step):
        pairs = []
        for i in range(peers):
            mine = i % PLANE
            if step is None:
                pairs.append((i, i ^ flip))
            elif mine in step and 0 <= i + PLANE * step[mine] < peers:
                pairs.append((i, (i ^ flip) + PLANE * step[mine]))
        return lax.ppermute(value, "chan", pairs)

    out = {0: -1, 1: -1, 2: 1, 3: 1}
    relay = {0: 1, 1: 1, 2: -1, 3: -1}
    inner = {1: 1, 2: -1}

    half = windows // 2
    part = functools.partial(whiten, record, rows, own_mask)
    t2a, t3a = part(q ^ 2, 0, half), part(q ^ 3, 0, half)
    t0, t1 = part(q, 0, windows), part(q ^ 1, 0, windows)
    t2b, t3b = part(q ^ 2, half, half), part(q ^ 3, half, half)
    y2a, y3a = send(t2a, 2, None), send(t3a, 3, None)
    z0, z1 = send(t0, 0, out), send(t1, 1, out)
    ea, eb = send(t0, 0, inner), send(t1, 1, inner)
    d2b, d3b = send(t2b, 2, out), send(t3b, 3, out)
    u1 = send(t1, 1, None)
    y2a, y3a, t2b, t3b = lax.optimization_barrier((y2a, y3a, t2b, t3b))
    s2a, s3a = send(y2a, 0, relay), send(y3a, 0, relay)
    y2b, y3b = send(t2b, 2, None), send(t3b, 3, None)

    g0, g1, g2, g3, s0, s1, d0, d1, extra = correlate(
        place, counts, jnp.asarray(tables), (t0, u1, y2a, y2b, y3a, y3b, z0, z1, s2a, d2b, s3a, d3b, ea, eb))

    to_x = {0: 1, 1: 1, 2: -1, 3: -1}
    to_v = {0: -1, 1: -1, 2: 1, 3: 1}
    parts = (
        g0, send(g1, 1, None), send(g2, 2, None), send(g3, 3, None),
        send(s0, 0, to_x), send(s1, 1, to_x), send(d0, 2, to_v), send(d1, 3, to_v),
        send(extra, 0, {1: -1, 2: 1}), send(extra, 1, {0: -1, 3: 1}),
    )
    return tuple(assemble(place, parts, (MAXP, lags // 2, width)))


def solution(mesh):
    return jax.shard_map(
        local,
        mesh=mesh,
        in_specs=(P(("grp", "chan"), None, None, None), P("grp", None), P("grp")),
        out_specs=(P(("grp", "chan"), None, None, None), P(("grp", "chan"), None, None, None)),
        check_vma=False,
    )
```

```python
import functools
import math

import jax
import jax.numpy as jnp
import numpy as np
from jax import lax
from jax.experimental import pallas as pl
from jax.experimental.pallas import tpu as pltpu
from jax.sharding import PartitionSpec as P

MAXP = 5
PLANE = 4
VMEM = 56 * 1024 * 1024
ROWS = 16
CHUNKS = 2

BASE = (
    ((0, 4), (0, 5), (1, 4), (1, 5), (0, 1)),
    ((0, 2), (0, 3), (1, 2), (1, 3), (2, 3)),
    ((3, 5), (-3, 2)),
)
OUTER = (((-1, 0), (-1, 2), (-1, 3), (-1, 4)),)
INNER = (((-2, 0), (-2, 1), (-2, 2), (-2, 3)),)
ALL = BASE + OUTER + INNER
DESTS = ((0, 1), (2, 3), (4, 5), (-2, -1), (None, -3))


def flat(groups):
    return [pair for group in groups for pair in group]


PAIRS = flat(ALL)


def items(spot):
    ahead = sorted(("ahead", b - a - 1) for a, b in PAIRS if a == spot)
    back = sorted(("back", b - a - 1) for a, b in PAIRS if b == spot)
    return ahead + back


SIZES = [max(len(items(spot)) for spot in spots) for spots in DESTS]
STARTS = [sum(SIZES[:d]) for d in range(len(SIZES))]
PLACE = {spot: (d, i) for d, spots in enumerate(DESTS) for i, spot in enumerate(spots)}


def lag_tables(lags):
    bins = lags // 2
    phase = (np.arange(lags)[:, None] * np.arange(1, bins + 1)[None, :] % lags) * (2.0 * math.pi / lags)
    real, imag = np.cos(phase), -np.sin(phase)
    causal = np.concatenate([real, imag], axis=1)
    other = np.concatenate([real, -imag], axis=1)
    near = np.concatenate([causal[:bins], causal[bins:][::-1]], axis=0)
    far = np.concatenate([other[bins:][::-1], other[:bins]], axis=0)
    return causal.astype(jnp.bfloat16), np.stack([near, far]).astype(jnp.bfloat16)


def whereabouts():
    me = lax.axis_index("chan").astype(jnp.int32)
    q = lax.rem(me, PLANE)
    far = q // 2
    return far, lax.rem(q, 2) ^ far, me - q, q


def whiten_body(mask_ref, table_ref, traces_ref, t0, t1, t2, t3, white, sems):
    outs = (t0, t1, t2, t3)
    _, _, base, q = whereabouts()
    bins = table_ref.shape[0] // 2
    part = white.shape[-1]
    step = traces_ref.shape[0]
    at = pl.program_id(0)
    for n in range(step):
        w = at * step + n
        raw = jnp.dot(table_ref[...], traces_ref[n], preferred_element_type=jnp.float32)
        power = jnp.sum(raw * raw, axis=0, keepdims=True) / bins
        valid = mask_ref[base + q, w].astype(jnp.float32)
        scaled = (raw * (valid * lax.rsqrt(power + 1e-06))).astype(jnp.bfloat16)
        for quarter in range(PLANE):
            piece = scaled[:, quarter * part:(quarter + 1) * part]
            white[quarter ^ q, w, 0] = piece[:bins]
            white[quarter ^ q, w, 1] = piece[bins:]

    def copy(k, i):
        span = pl.ds(i * step, step)
        return pltpu.make_async_copy(white.at[k, span], outs[k].at[span], sems.at[k, i])

    for k in range(PLANE):
        copy(k, at).start()

    @pl.when(at == pl.num_programs(0) - 1)
    def _():
        for k in range(PLANE):
            for i in range(sems.shape[1]):
                copy(k, i).wait()


def whiten(mask, table, record):
    windows, lags, width = record.shape
    bins = lags // 2
    part = width // PLANE
    step = 4
    return pl.pallas_call(
        whiten_body,
        grid=(windows // step,),
        in_specs=[
            pl.BlockSpec(memory_space=pltpu.SMEM),
            pl.BlockSpec((lags, lags), lambda i: (0, 0)),
            pl.BlockSpec((step, lags, width), lambda i: (i, 0, 0)),
        ],
        out_specs=[pl.BlockSpec(memory_space=pl.ANY)] * PLANE,
        out_shape=[jax.ShapeDtypeStruct((windows, 2, bins, part), jnp.bfloat16)] * PLANE,
        scratch_shapes=[
            pltpu.VMEM((PLANE, windows, 2, bins, part), jnp.bfloat16),
            pltpu.SemaphoreType.DMA((PLANE, windows // step)),
        ],
        compiler_params=pltpu.CompilerParams(vmem_limit_bytes=VMEM),
        cost_estimate=pl.CostEstimate(flops=2 * windows * lags * lags * width, bytes_accessed=4 * windows * lags * width, transcendentals=0),
    )(mask, table, record)


def on(m, mine):
    return (lambda body: body()) if mine is None else pl.when(m == mine)


def correlate_body(counts_ref, table_ref, *refs, work, slots, loads, late):
    ins, refs = refs[:len(loads)], refs[len(loads) + late * (len(DESTS) + 1):]
    outs, refs = refs[:len(DESTS) + 1], refs[len(DESTS) + 1:]
    blocks_ref, stack, kept, sems, out_sems = refs[0], refs[1], refs[2:2 + len(DESTS)], refs[-2], refs[-1]
    windows, _, bins, part = ins[0].shape
    far, m, base, _ = whereabouts()
    blocks = counts_ref.shape[0]
    chunk = bins // CHUNKS

    waits = [[] for _ in range(CHUNKS)]
    for c in range(CHUNKS):
        span = pl.ds(c * chunk, chunk)
        for n, both in enumerate(loads):
            there = [s for s in both if s is not None]
            mine = None if len(there) == 2 else both.index(there[0])
            slot = there[0] + m * (there[-1] - there[0])
            one = pltpu.make_async_copy(ins[n].at[:, :, span], blocks_ref.at[slot, :, :, span], sems.at[n, c])
            on(m, mine)(one.start)
            waits[c].append((mine, one))

    scale = 1.0 / math.sqrt(windows)
    begin = [sum(len(flat(groups)) for _, groups in work[:n]) for n in range(len(work))]

    def sum_up(group, at, c):
        need = sorted({spot for pair in group for spot in pair})

        def tile(kt, carry):
            top = pl.multiple_of(kt * ROWS, ROWS)
            rows = pl.ds(top, ROWS)

            def window(w, sums):
                real = {s: blocks_ref[slots[s], w, 0, rows, :].astype(jnp.float32) for s in need}
                imag = {s: blocks_ref[slots[s], w, 1, rows, :].astype(jnp.float32) for s in need}
                out = []
                for n, (a, b) in enumerate(group):
                    out.append(sums[2 * n] + (real[a] * real[b] + imag[a] * imag[b]))
                    out.append(sums[2 * n + 1] + (imag[a] * real[b] - real[a] * imag[b]))
                return tuple(out)

            zero = jnp.zeros((ROWS, part), jnp.float32)
            sums = lax.fori_loop(0, windows, window, (zero,) * (2 * len(group)), unroll=8)
            for n in range(len(group)):
                lanes = pl.ds((at + n) * part, part)
                stack[rows, lanes] = (sums[2 * n] * scale).astype(jnp.bfloat16)
                stack[pl.ds(pl.multiple_of(bins + top, ROWS), ROWS), lanes] = (sums[2 * n + 1] * scale).astype(jnp.bfloat16)
            return carry

        lax.fori_loop(c * chunk // ROWS, (c + 1) * chunk // ROWS, tile, 0)

    norm = 1.0 / math.sqrt(bins)

    def to_lags(groups, at):
        for n, (a, b) in enumerate(flat(groups), at):
            corr = jnp.dot(table_ref[far], stack[:, n * part:(n + 1) * part], preferred_element_type=jnp.float32)
            first = jnp.where(far == 0, base + a, base + 3 - b)
            reach = counts_ref[jnp.clip(first, 0, blocks - 1)]
            corr = corr * jnp.where(reach >= b - a, norm, 0.0)
            for spot, kind, rows in ((a, "ahead", corr[:bins]), (b, "back", corr[bins:])):
                d, i = PLACE[spot]
                kept[d][i, items(spot).index((kind, b - a - 1))] = rows.astype(jnp.bfloat16)

    for c in range(CHUNKS):
        for mine, one in waits[c]:
            on(m, mine)(one.wait)
        for n, (mine, groups) in enumerate(work):
            @on(m, mine)
            def _(at=begin[n], groups=groups):
                for g, group in enumerate(groups):
                    sum_up(group, at + len(flat(groups[:g])), c)

    for n, (mine, groups) in enumerate(work):
        @on(m, mine)
        def _(at=begin[n], mine=mine, groups=groups):
            to_lags(groups, at)
            if not late:
                return
            copies = []
            for a, b in flat(groups):
                for spot, kind in ((a, "ahead"), (b, "back")):
                    d, i = PLACE[spot]
                    row = items(spot).index((kind, b - a - 1))
                    target = outs[d].at[row] if i == mine else outs[-1].at[STARTS[d] + row]
                    copies.append(pltpu.make_async_copy(kept[d].at[i, row], target, out_sems.at[len(copies)]))
            for one in copies:
                one.start()
            for one in copies:
                one.wait()

    if not late:
        copies = []
        for d, size in enumerate(SIZES):
            copies.append(pltpu.make_async_copy(kept[d].at[m], outs[d].at[pl.ds(0, size)], out_sems.at[2 * d]))
            copies.append(pltpu.make_async_copy(kept[d].at[1 - m], outs[-1].at[pl.ds(STARTS[d], size)], out_sems.at[2 * d + 1]))
        for one in copies:
            one.start()
        for one in copies:
            one.wait()


def correlate(counts, tables, whites, work, slots, loads, filled=()):
    windows, _, bins, part = whites[0].shape
    most = max(sum(len(flat(groups)) for mine, groups in work if mine in (None, m)) for m in range(2))
    widest = sum(len(flat(groups)) for _, groups in work)
    anywhere = pl.BlockSpec(memory_space=pl.ANY)
    scalars = pl.BlockSpec(memory_space=pltpu.SMEM)
    lengths = [SIZES[0]] + [2 * size for size in SIZES[1:]] + [sum(SIZES)]
    return pl.pallas_call(
        functools.partial(correlate_body, work=work, slots=slots, loads=loads, late=bool(filled)),
        in_specs=[scalars, pl.BlockSpec(memory_space=pltpu.VMEM)] + [anywhere] * (len(whites) + len(filled)),
        out_specs=[anywhere] * len(lengths),
        out_shape=[jax.ShapeDtypeStruct((n, bins, part), jnp.bfloat16) for n in lengths],
        scratch_shapes=[
            pltpu.VMEM((max(slots.values()) + 1, windows, 2, bins, part), jnp.bfloat16),
            pltpu.VMEM((2 * bins, widest * part), jnp.bfloat16),
            *[pltpu.VMEM((2, size, bins, part), jnp.bfloat16) for size in SIZES],
            pltpu.SemaphoreType.DMA((len(whites), CHUNKS)),
            pltpu.SemaphoreType.DMA((2 * max(len(DESTS), most),)),
        ],
        input_output_aliases={2 + len(whites) + i: i for i in range(len(filled))},
        compiler_params=pltpu.CompilerParams(vmem_limit_bytes=VMEM),
        cost_estimate=pl.CostEstimate(flops=100 * most * windows * bins * part, bytes_accessed=4 * len(whites) * windows * bins * part, transcendentals=0),
    )(counts, tables, *whites, *filled)


def merge_body(sib, *refs):
    outs, sems = refs[len(DESTS) - 1:-1], refs[-1]
    copies = []
    for d in range(1, len(DESTS)):
        copies.append(pltpu.make_async_copy(
            sib.at[pl.ds(STARTS[d], SIZES[d])], outs[d - 1].at[pl.ds(SIZES[d], SIZES[d])], sems.at[d - 1]))
    for one in copies:
        one.start()
    for one in copies:
        one.wait()


def merge(sib, own):
    anywhere = pl.BlockSpec(memory_space=pl.ANY)
    return pl.pallas_call(
        merge_body,
        in_specs=[pl.BlockSpec(memory_space=pltpu.VMEM)] + [anywhere] * len(own),
        out_specs=[anywhere] * len(own),
        out_shape=[jax.ShapeDtypeStruct(value.shape, value.dtype) for value in own],
        scratch_shapes=[pltpu.SemaphoreType.DMA((len(own),))],
        input_output_aliases={1 + i: i for i in range(len(own))},
    )(sib, *own)


def assemble_body(*refs, plan, count, filled):
    ins, refs = refs[:count], refs[count + 2 * filled:]
    forward, backward, wide, sems = refs
    far, m, _, q = whereabouts()
    part = ins[0].shape[2]
    for mine in range(2):
        @pl.when(m == mine)
        def _(mine=mine):
            waits = []
            for a, k, spot, first in plan[mine]:
                lanes = pl.ds(pl.multiple_of((q ^ k) * part, part), part)
                ahead = far if k < 2 else 1 - far
                for n, (kind, j) in enumerate(items(spot)):
                    at = len(waits)
                    wide[at] = ins[a][first + n].astype(jnp.float32)
                    side = ahead if kind == "ahead" else 1 - ahead
                    copies = [pltpu.make_async_copy(wide.at[at], ref.at[0, j, :, lanes], sems.at[at]) for ref in (forward, backward)]
                    for value, copy in enumerate(copies):
                        pl.when(side == value)(copy.start)
                    waits.append(copies[0])
            for copy in waits:
                copy.wait()


def assemble(parts, shape, plan, filled=()):
    steps = max(sum(len(items(spot)) for _, _, spot, _ in one) for one in plan)
    anywhere = pl.BlockSpec(memory_space=pl.ANY)
    bins, part = parts[0].shape[1:]
    return pl.pallas_call(
        functools.partial(assemble_body, plan=plan, count=len(parts), filled=len(filled) // 2),
        in_specs=[pl.BlockSpec(memory_space=pltpu.VMEM)] * len(parts) + [anywhere] * len(filled),
        out_specs=[anywhere] * 2,
        out_shape=[jax.ShapeDtypeStruct((1,) + shape, jnp.float32)] * 2,
        scratch_shapes=[pltpu.VMEM((steps, bins, part), jnp.float32), pltpu.SemaphoreType.DMA((steps,))],
        input_output_aliases={len(parts) + i: i for i in range(len(filled))},
        compiler_params=pltpu.CompilerParams(vmem_limit_bytes=VMEM),
        cost_estimate=pl.CostEstimate(flops=steps * bins * part, bytes_accessed=6 * steps * bins * part, transcendentals=0),
    )(*parts, *filled)


HERE = (0, 0, 0, 0)
OUTWARD = (-1, -1, 1, 1)
INWARD = (1, 1, -1, -1)
INNER_INWARD = (None, 1, -1, None)
INNER_OUTWARD = (None, -1, 1, None)


def send(value, flip, step):
    peers = lax.axis_size("chan")
    pairs = []
    for i in range(peers):
        planes = step[i % PLANE]
        if planes is not None and 0 <= i + PLANE * planes < peers:
            pairs.append((i, (i ^ flip) + PLANE * planes))
    return lax.ppermute(value, "chan", pairs)


def after(value, *done):
    return lax.optimization_barrier((value,) + done)[0]


def local(traces, mask, counts):
    record = traces[0]
    windows, lags, width = record.shape
    causal, tables = lag_tables(lags)
    tables = jnp.asarray(tables)
    t0, t1, t2, t3 = whiten(mask, jnp.asarray(np.ascontiguousarray(causal.T)), record)

    y2, y3 = send(t2, 2, HERE), send(t3, 3, HERE)
    z0 = send(t0, 0, OUTWARD)
    ea, eb = send(t0, 0, INNER_INWARD), send(t1, 1, INNER_INWARD)
    t1 = after(t1, z0)
    z1, u1 = send(t1, 1, OUTWARD), send(t1, 1, HERE)
    r2, r3 = send(after(y2, ea, eb), 0, INWARD), send(y3, 0, INWARD)

    parts = correlate(
        counts, tables, (t0, u1, y2, y3, z0, z1, eb, ea, r2), ((None, BASE), (0, INNER), (1, OUTER)),
        slots={0: 0, 1: 1, 2: 2, 3: 3, 4: 4, 5: 5, -3: 6, -2: 7, -1: 7},
        loads=((0, 1), (1, 0), (2, 3), (3, 2), (4, 5), (5, 4), (6, None), (None, 6), (7, 7)))
    keep, f, x, v, w, sib = correlate(
        counts, tables, (t0, u1, y2, y3, z0, r3), ((0, OUTER), (1, INNER)),
        slots={0: 0, 1: 1, 2: 2, 3: 3, 4: 4, -2: 5, -1: 5},
        loads=((0, 1), (1, 0), (2, 3), (3, 2), (4, None), (5, 5)), filled=parts)

    sib = send(sib, 1, HERE)
    f, x, v, w = merge(sib, (f, x, v, w))
    f, x, v = send(f, 2, HERE), send(x, 0, INWARD), send(v, 2, OUTWARD)
    w = send(w, 0, INNER_OUTWARD)

    shape = (MAXP, lags // 2, width)
    filled = assemble((keep, sib), shape, [[(0, 0, mine, 0), (1, 1, mine, 0)] for mine in range(2)])
    return tuple(assemble((f, x, v, w), shape, [
        [(0, 2, 3 - mine, 0), (0, 3, 3 - mine, SIZES[1]), (1, 0, 4 + mine, 0), (1, 1, 4 + mine, SIZES[2]),
         (2, 2, -1 - mine, 0), (2, 3, -1 - mine, SIZES[3])] + inner
        for mine, inner in enumerate(([], [(3, 0, -3, 0), (3, 1, -3, 1)]))], filled))


def solution(mesh):
    return jax.shard_map(
        local,
        mesh=mesh,
        in_specs=(P(("grp", "chan"), None, None, None), P("grp", None), P("grp")),
        out_specs=(P(("grp", "chan"), None, None, None), P(("grp", "chan"), None, None, None)),
        check_vma=False,
    )
```

```python
import functools
import math

import jax
import jax.numpy as jnp
import numpy as np
from jax import lax
from jax.experimental import pallas as pl
from jax.experimental.pallas import tpu as pltpu
from jax.sharding import PartitionSpec as P

MAXP = 5
PLANE = 4
MIB = 1024 * 1024
ROWS = 16
STEP = 8

NEAR = (((0, 1), (0, 2), (1, 2)), ((0, 1), (0, 3), (1, 3)))
REST = (((0, 3), (1, 3), (2, 3)), ((0, 2), (1, 2), (2, 3)))
FIRST = ((-3, 2),)
BEYOND = ((0, 4), (0, 5), (1, 4), (1, 5), (3, 5))
OUTER = ((-1, 0), (-1, 2), (-1, 3), (-1, 4))
INNER = ((-2, 0), (-2, 1), (-2, 2), (-2, 3))
PAIRS = NEAR[0] + REST[0] + FIRST + BEYOND + OUTER + INNER
DESTS = ((0, 1), (2, 3), (4, 5), (-2, -1), (None, -3))


def flat(groups):
    return [pair for group in groups for pair in group]


def items(spot):
    ahead = sorted(("ahead", b - a - 1) for a, b in PAIRS if a == spot)
    back = sorted(("back", b - a - 1) for a, b in PAIRS if b == spot)
    return ahead + back


SIZES = [max(len(items(spot)) for spot in spots) for spots in DESTS]
STARTS = [sum(SIZES[:d]) for d in range(len(SIZES))]
PLACE = {spot: (d, i) for d, spots in enumerate(DESTS) for i, spot in enumerate(spots)}


def lag_tables(lags):
    bins = lags // 2
    phase = (np.arange(lags)[:, None] * np.arange(1, bins + 1)[None, :] % lags) * (2.0 * math.pi / lags)
    real, imag = np.cos(phase), -np.sin(phase)
    causal = np.concatenate([real, imag], axis=1)
    other = np.concatenate([real, -imag], axis=1)
    near = np.concatenate([causal[:bins], causal[bins:][::-1]], axis=0)
    far = np.concatenate([other[bins:][::-1], other[:bins]], axis=0)
    return causal.astype(jnp.bfloat16), np.stack([near, far]).astype(jnp.bfloat16)


def whereabouts():
    me = lax.axis_index("chan").astype(jnp.int32)
    q = lax.rem(me, PLANE)
    far = q // 2
    return far, lax.rem(q, 2) ^ far, me - q, q


def whiten_body(mask_ref, table_ref, traces_ref, *refs):
    outs, (white, sems) = refs[:-2], refs[-2:]
    _, _, base, q = whereabouts()
    windows = white.shape[1]
    bins = table_ref.shape[0] // 2
    part = white.shape[-1]
    step = traces_ref.shape[1]
    at = pl.program_id(0)
    for n in range(step):
        w = at * step + n
        raw = jnp.dot(table_ref[...], traces_ref[0, n], preferred_element_type=jnp.float32)
        power = jnp.sum(raw * raw, axis=0, keepdims=True) / bins
        valid = mask_ref[base + q, w].astype(jnp.float32)
        scaled = (raw * (valid * lax.rsqrt(power + 1e-06))).astype(jnp.bfloat16)
        for quarter in range(2):
            piece = scaled[:, quarter * part:(quarter + 1) * part]
            white[quarter ^ lax.rem(q, 2), w, 0] = piece[:bins]
            white[quarter ^ lax.rem(q, 2), w, 1] = piece[bins:]

    def copies(i):
        span = pl.ds(i * step, step)
        targets = (outs[0].at[span], outs[0].at[pl.ds(windows + i * step, step)]) if len(outs) == 1 else [out.at[span] for out in outs]
        return [pltpu.make_async_copy(white.at[k, span], target, sems.at[k, i]) for k, target in enumerate(targets)]

    for one in copies(at):
        one.start()

    @pl.when(at == pl.num_programs(0) - 1)
    def _():
        for i in range(sems.shape[1]):
            for one in copies(i):
                one.wait()


def whiten(mask, table, traces, lengths):
    _, windows, lags, width = traces.shape
    bins = lags // 2
    part = width // PLANE
    other = len(lengths) - 1

    def half(i):
        far = whereabouts()[0]
        return 0, i, 0, 1 - far if other else far

    return pl.pallas_call(
        whiten_body,
        grid=(windows // STEP,),
        in_specs=[
            pl.BlockSpec(memory_space=pltpu.SMEM),
            pl.BlockSpec((lags, lags), lambda i: (0, 0)),
            pl.BlockSpec((1, STEP, lags, 2 * part), half),
        ],
        out_specs=[pl.BlockSpec(memory_space=pl.ANY)] * len(lengths),
        out_shape=[jax.ShapeDtypeStruct((n, 2, bins, part), jnp.bfloat16) for n in lengths],
        scratch_shapes=[
            pltpu.VMEM((2, windows, 2, bins, part), jnp.bfloat16),
            pltpu.SemaphoreType.DMA((2, windows // STEP)),
        ],
        compiler_params=pltpu.CompilerParams(vmem_limit_bytes=57 * MIB),
        cost_estimate=pl.CostEstimate(flops=windows * lags * lags * width, bytes_accessed=2 * windows * lags * width, transcendentals=0),
    )(mask, table, traces)


def relayed(windows):
    return windows * 5 // 8


def correlate_body(counts_ref, table_ref, *refs, work, sources, filled):
    ins, refs = refs[:len(refs) - 2 * len(DESTS) - 3 - filled], refs[len(refs) - 2 * len(DESTS) - 3:]
    outs, stack, kept, out_sems = refs[:len(DESTS) + 1], refs[len(DESTS) + 1], refs[len(DESTS) + 2:-1], refs[-1]
    windows, _, bins, part = ins[1].shape
    far, m, base, _ = whereabouts()
    blocks = counts_ref.shape[0]
    scale = 1.0 / math.sqrt(windows)
    norm = 1.0 / math.sqrt(bins)

    def sum_up(group, at, where):
        need = sorted({spot for pair in group for spot in pair})
        edges = sorted({edge for s in need for _, start, stop in where[s] for edge in (start, stop)})

        def tile(kt, carry):
            top = pl.multiple_of(kt * ROWS, ROWS)
            rows = pl.ds(top, ROWS)
            sums = (jnp.zeros((ROWS, part), jnp.float32),) * (2 * len(group))
            for start, stop in zip(edges, edges[1:]):
                def window(w, sums, start=start):
                    real, imag = {}, {}
                    for s in need:
                        array, begin = [(a, start - first) for a, first, last in where[s] if first <= start < last][0]
                        real[s] = ins[array][begin + w, 0, rows, :].astype(jnp.float32)
                        imag[s] = ins[array][begin + w, 1, rows, :].astype(jnp.float32)
                    out = []
                    for n, (a, b) in enumerate(group):
                        out.append(sums[2 * n] + (real[a] * real[b] + imag[a] * imag[b]))
                        out.append(sums[2 * n + 1] + (imag[a] * real[b] - real[a] * imag[b]))
                    return tuple(out)

                sums = lax.fori_loop(0, stop - start, window, sums, unroll=math.gcd(stop - start, 8))
            for n in range(len(group)):
                lanes = pl.ds((at + n) * part, part)
                stack[rows, lanes] = (sums[2 * n] * scale).astype(jnp.bfloat16)
                stack[pl.ds(pl.multiple_of(bins + top, ROWS), ROWS), lanes] = (sums[2 * n + 1] * scale).astype(jnp.bfloat16)
            return carry

        lax.fori_loop(0, bins // ROWS, tile, 0)

    for mine in range(2):
        @pl.when(m == mine)
        def _(mine=mine):
            copies = []
            for g, group in enumerate(work[mine]):
                at = len(flat(work[mine][:g]))
                sum_up(group, at, sources[mine])
                lags = jnp.dot(table_ref[far], stack[:, at * part:(at + len(group)) * part], preferred_element_type=jnp.float32)
                for n, (a, b) in enumerate(group):
                    first = jnp.where(far == 0, base + a, base + 3 - b)
                    reach = counts_ref[jnp.clip(first, 0, blocks - 1)]
                    corr = lags[:, n * part:(n + 1) * part] * jnp.where(reach >= b - a, norm, 0.0)
                    for spot, kind, rows in ((a, "ahead", corr[:bins]), (b, "back", corr[bins:])):
                        d, i = PLACE[spot]
                        row = items(spot).index((kind, b - a - 1))
                        kept[d][i, row] = rows.astype(jnp.bfloat16)
                        target = outs[d].at[row] if i == mine else outs[-1].at[STARTS[d] + row]
                        one = pltpu.make_async_copy(kept[d].at[i, row], target, out_sems.at[len(copies)])
                        one.start()
                        copies.append(one)
            for one in copies:
                one.wait()


def correlate(counts, tables, whites, work, sources, filled=(), weight=1):
    windows, _, bins, part = whites[1].shape
    most = max(len(flat(groups)) for groups in work)
    anywhere = pl.BlockSpec(memory_space=pl.ANY)
    scalars = pl.BlockSpec(memory_space=pltpu.SMEM)
    lengths = [SIZES[0]] + [2 * size for size in SIZES[1:]] + [sum(SIZES)]
    return pl.pallas_call(
        functools.partial(correlate_body, work=work, sources=sources, filled=len(filled)),
        in_specs=[scalars] + [pl.BlockSpec(memory_space=pltpu.VMEM)] * (1 + len(whites)) + [anywhere] * len(filled),
        out_specs=[anywhere] * len(lengths),
        out_shape=[jax.ShapeDtypeStruct((n, bins, part), jnp.bfloat16) for n in lengths],
        scratch_shapes=[
            pltpu.VMEM((2 * bins, most * part), jnp.bfloat16),
            *[pltpu.VMEM((2, size, bins, part), jnp.bfloat16) for size in SIZES],
            pltpu.SemaphoreType.DMA((2 * most,)),
        ],
        input_output_aliases={2 + len(whites) + i: i for i in range(len(filled))},
        compiler_params=pltpu.CompilerParams(vmem_limit_bytes=12 * MIB),
        cost_estimate=pl.CostEstimate(flops=weight * 100 * most * windows * bins * part, bytes_accessed=min(weight, 1) * 4 * len(whites) * windows * bins * part, transcendentals=0),
    )(counts, tables, *whites, *filled)


def merge_body(sib, *refs):
    outs, sems = refs[len(DESTS) - 1:-1], refs[-1]
    copies = []
    for d in range(1, len(DESTS)):
        copies.append(pltpu.make_async_copy(
            sib.at[pl.ds(STARTS[d], SIZES[d])], outs[d - 1].at[pl.ds(SIZES[d], SIZES[d])], sems.at[d - 1]))
    for one in copies:
        one.start()
    for one in copies:
        one.wait()


def merge(sib, own):
    anywhere = pl.BlockSpec(memory_space=pl.ANY)
    return pl.pallas_call(
        merge_body,
        in_specs=[pl.BlockSpec(memory_space=pltpu.VMEM)] + [anywhere] * len(own),
        out_specs=[anywhere] * len(own),
        out_shape=[jax.ShapeDtypeStruct(value.shape, value.dtype) for value in own],
        scratch_shapes=[pltpu.SemaphoreType.DMA((len(own),))],
        input_output_aliases={1 + i: i for i in range(len(own))},
        compiler_params=pltpu.CompilerParams(vmem_limit_bytes=4 * MIB),
    )(sib, *own)


def assemble_body(*refs, plan, count, filled):
    ins, refs = refs[:count], refs[count + 2 * filled:]
    forward, backward, wide, sems = refs
    far, m, _, q = whereabouts()
    part = ins[0].shape[2]
    for mine in range(2):
        @pl.when(m == mine)
        def _(mine=mine):
            waits = []
            for a, k, spot, first in plan[mine]:
                lanes = pl.ds(pl.multiple_of((q ^ k) * part, part), part)
                ahead = far if k < 2 else 1 - far
                for n, (kind, j) in enumerate(items(spot)):
                    at = len(waits)
                    wide[at] = ins[a][first + n].astype(jnp.float32)
                    side = ahead if kind == "ahead" else 1 - ahead
                    copies = [pltpu.make_async_copy(wide.at[at], ref.at[0, j, :, lanes], sems.at[at]) for ref in (forward, backward)]
                    for value, copy in enumerate(copies):
                        pl.when(side == value)(copy.start)
                    waits.append(copies[0])
            for copy in waits:
                copy.wait()


def assemble(parts, shape, plan, filled=()):
    steps = max(sum(len(items(spot)) for _, _, spot, _ in one) for one in plan)
    anywhere = pl.BlockSpec(memory_space=pl.ANY)
    bins, part = parts[0].shape[1:]
    return pl.pallas_call(
        functools.partial(assemble_body, plan=plan, count=len(parts), filled=len(filled) // 2),
        in_specs=[pl.BlockSpec(memory_space=pltpu.VMEM)] * len(parts) + [anywhere] * len(filled),
        out_specs=[anywhere] * 2,
        out_shape=[jax.ShapeDtypeStruct((1,) + shape, jnp.float32)] * 2,
        scratch_shapes=[pltpu.VMEM((steps, bins, part), jnp.float32), pltpu.SemaphoreType.DMA((steps,))],
        input_output_aliases={len(parts) + i: i for i in range(len(filled))},
        compiler_params=pltpu.CompilerParams(vmem_limit_bytes=12 * MIB),
        cost_estimate=pl.CostEstimate(flops=steps * bins * part, bytes_accessed=6 * steps * bins * part, transcendentals=0),
    )(*parts, *filled)


HERE = (0, 0, 0, 0)
OUTWARD = (-1, -1, 1, 1)
INWARD = (1, 1, -1, -1)
INNER_HERE = (None, 0, 0, None)
INNER_INWARD = (None, 1, -1, None)
INNER_OUTWARD = (None, -1, 1, None)


def send(value, flip, step):
    peers = lax.axis_size("chan")
    pairs = []
    for i in range(peers):
        planes = step[i % PLANE]
        if planes is not None and 0 <= i + PLANE * planes < peers:
            pairs.append((i, (i ^ flip) + PLANE * planes))
    return lax.ppermute(value, "chan", pairs)


def after(value, *done):
    return lax.optimization_barrier((value,) + done)[0]


def local(traces, mask, counts):
    _, windows, lags, width = traces.shape
    causal, tables = lag_tables(lags)
    tables = jnp.asarray(tables)
    rows = jnp.asarray(np.ascontiguousarray(causal.T))
    t2, t3 = whiten(mask, rows, traces, (windows, windows))
    t01, = whiten(after(mask, t2), rows, traces, (2 * windows,))

    y2, y3 = send(t2, 2, HERE), send(t3, 3, HERE)
    z, e = send(t01, 0, OUTWARD), send(t01, 0, INNER_INWARD)
    u1 = send(t01[windows:], 1, HERE)
    r2 = send(after(y2, u1), 0, INWARD)
    r3b = send(after(t3, y2)[relayed(windows):], 3, OUTWARD)

    whole = lambda *arrays: {spot: ((array, 0, windows),) for spot, array in arrays}
    parts = correlate(
        counts, tables, (t01, u1, y2), ((NEAR[0],), (NEAR[1],)), sources=(
            whole((0, 0), (1, 1), (2, 2)),
            whole((0, 1), (1, 0), (3, 2))), weight=200)
    r3a = send(after(y3, parts[4])[:relayed(windows)], 0, INWARD)
    e1 = send(after(e, parts[4])[windows:], 1, INNER_HERE)
    parts = correlate(
        counts, tables, (t01, u1, y2, y3), ((REST[0],), (REST[1],)), sources=(
            whole((0, 0), (1, 1), (2, 2), (3, 3)),
            whole((0, 1), (1, 0), (2, 3), (3, 2))), filled=parts, weight=200)
    half = windows // 2
    z = after(z, parts[4])
    z1a, z1b = send(z[windows:windows + half], 1, HERE), send(z[windows + half:], 1, HERE)
    other = ((5, 0, half), (6, half, windows))
    parts = correlate(
        counts, tables, (t01, u1, y2, y3, z, z1a, z1b, r2, e1, e), ((BEYOND, INNER, FIRST), (BEYOND, OUTER, FIRST)), sources=(
            whole((0, 0), (1, 1), (2, 2), (3, 3), (4, 4), (-2, 7), (-3, 8)) | {5: other},
            whole((0, 1), (1, 0), (2, 3), (3, 2), (5, 4), (-1, 7), (-3, 9)) | {4: other}), filled=parts, weight=0)
    last = ((5, 0, relayed(windows)), (6, relayed(windows), windows))
    keep, f, x, v, w, sib = correlate(
        counts, tables, (t01, u1, y2, y3, z, r3a, r3b), ((OUTER,), (INNER,)), sources=(
            whole((0, 0), (1, 1), (2, 2), (3, 3), (4, 4)) | {-1: last},
            whole((0, 1), (1, 0), (2, 3), (3, 2)) | {-2: last}), filled=parts)

    sib = send(sib, 1, HERE)
    f, x, v, w = merge(sib, (f, x, v, w))
    f, x, v = send(f, 2, HERE), send(x, 0, INWARD), send(v, 2, OUTWARD)
    w = send(w, 0, INNER_OUTWARD)

    shape = (MAXP, lags // 2, width)
    filled = assemble((keep, sib), shape, [[(0, 0, mine, 0), (1, 1, mine, 0)] for mine in range(2)])
    return tuple(assemble((f, x, v, w), shape, [
        [(0, 2, 3 - mine, 0), (0, 3, 3 - mine, SIZES[1]), (1, 0, 4 + mine, 0), (1, 1, 4 + mine, SIZES[2]),
         (2, 2, -1 - mine, 0), (2, 3, -1 - mine, SIZES[3])] + inner
        for mine, inner in enumerate(([], [(3, 0, -3, 0), (3, 1, -3, 1)]))], filled))


def solution(mesh):
    return jax.shard_map(
        local,
        mesh=mesh,
        in_specs=(P(("grp", "chan"), None, None, None), P("grp", None), P("grp")),
        out_specs=(P(("grp", "chan"), None, None, None), P(("grp", "chan"), None, None, None)),
        check_vma=False,
    )
```

```python
import functools
import math

import jax
import jax.numpy as jnp
import numpy as np
from jax import lax
from jax.experimental import pallas as pl
from jax.experimental.pallas import tpu as pltpu
from jax.sharding import PartitionSpec as P

MAXP = 5
PLANE = 4
MIB = 1024 * 1024
ROWS = 16
STEP = 8

NEAR = (((0, 1), (0, 2), (1, 2)), ((0, 1), (0, 3), (1, 3)))
REST = (((0, 3), (1, 3), (2, 3)), ((0, 2), (1, 2), (2, 3)))
FIRST = ((-3, 2),)
BEYOND = ((0, 4), (0, 5), (1, 4), (1, 5), (3, 5))
OUTER = ((-1, 0), (-1, 2), (-1, 3), (-1, 4))
INNER = ((-2, 0), (-2, 1), (-2, 2), (-2, 3))
PAIRS = NEAR[0] + REST[0] + FIRST + BEYOND + OUTER + INNER
DESTS = ((0, 1), (2, 3), (4, 5), (-2, -1), (None, -3))


def flat(groups):
    return [pair for group in groups for pair in group]


def items(spot):
    ahead = sorted(("ahead", b - a - 1) for a, b in PAIRS if a == spot)
    back = sorted(("back", b - a - 1) for a, b in PAIRS if b == spot)
    return ahead + back


MERGED = (2, 3, 4)
SIZES = [max(len(items(spot)) for spot in spots) for spots in DESTS]
STARTS = [sum(SIZES[:d]) for d in range(len(SIZES))]
PLACE = {spot: (d, i) for d, spots in enumerate(DESTS) for i, spot in enumerate(spots)}


def lag_tables(lags):
    bins = lags // 2
    phase = (np.arange(lags)[:, None] * np.arange(1, bins + 1)[None, :] % lags) * (2.0 * math.pi / lags)
    real, imag = np.cos(phase), -np.sin(phase)
    causal = np.concatenate([real, imag], axis=1)
    other = np.concatenate([real, -imag], axis=1)
    near = np.concatenate([causal[:bins], causal[bins:][::-1]], axis=0)
    far = np.concatenate([other[bins:][::-1], other[:bins]], axis=0)
    return causal.astype(jnp.bfloat16), np.stack([near, far]).astype(jnp.bfloat16)


def whereabouts():
    me = lax.axis_index("chan").astype(jnp.int32)
    q = lax.rem(me, PLANE)
    far = q // 2
    return far, lax.rem(q, 2) ^ far, me - q, q


def whiten_body(mask_ref, table_ref, traces_ref, *refs):
    outs, (white, sems) = refs[:-2], refs[-2:]
    _, _, base, q = whereabouts()
    windows = white.shape[1]
    bins = table_ref.shape[0] // 2
    part = white.shape[-1]
    step = traces_ref.shape[1]
    at = pl.program_id(0)
    for n in range(step):
        w = at * step + n
        raw = jnp.dot(table_ref[...], traces_ref[0, n], preferred_element_type=jnp.float32)
        power = jnp.sum(raw * raw, axis=0, keepdims=True) / bins
        valid = mask_ref[base + q, w].astype(jnp.float32)
        scaled = (raw * (valid * lax.rsqrt(power + 1e-06))).astype(jnp.bfloat16)
        for quarter in range(2):
            piece = scaled[:, quarter * part:(quarter + 1) * part]
            white[quarter ^ lax.rem(q, 2), w, 0] = piece[:bins]
            white[quarter ^ lax.rem(q, 2), w, 1] = piece[bins:]

    def copies(i):
        span = pl.ds(i * step, step)
        targets = [(n, out.at[span]) for n, out in enumerate(outs)]
        if outs[0].shape[0] > windows:
            targets.append((1, outs[0].at[pl.ds(windows + i * step, step)]))
        return [pltpu.make_async_copy(white.at[k, span], target, sems.at[n, i]) for n, (k, target) in enumerate(targets)]

    for one in copies(at):
        one.start()

    @pl.when(at == pl.num_programs(0) - 1)
    def _():
        for i in range(sems.shape[1]):
            for one in copies(i):
                one.wait()


def whiten(mask, table, traces, lengths):
    _, windows, lags, width = traces.shape
    bins = lags // 2
    part = width // PLANE
    other = lengths[0] == windows

    def half(i):
        far = whereabouts()[0]
        return 0, i, 0, 1 - far if other else far

    return pl.pallas_call(
        whiten_body,
        grid=(windows // STEP,),
        in_specs=[
            pl.BlockSpec(memory_space=pltpu.SMEM),
            pl.BlockSpec((lags, lags), lambda i: (0, 0)),
            pl.BlockSpec((1, STEP, lags, 2 * part), half),
        ],
        out_specs=[pl.BlockSpec(memory_space=pl.ANY)] * len(lengths),
        out_shape=[jax.ShapeDtypeStruct((n, 2, bins, part), jnp.bfloat16) for n in lengths],
        scratch_shapes=[
            pltpu.VMEM((2, windows, 2, bins, part), jnp.bfloat16),
            pltpu.SemaphoreType.DMA((3, windows // STEP)),
        ],
        compiler_params=pltpu.CompilerParams(vmem_limit_bytes=57 * MIB),
        cost_estimate=pl.CostEstimate(flops=windows * lags * lags * width, bytes_accessed=2 * windows * lags * width, transcendentals=0),
    )(mask, table, traces)


def relayed(windows):
    return windows * 5 // 8


def correlate_body(counts_ref, table_ref, *refs, work, sources, filled):
    ins, refs = refs[:len(refs) - 2 * len(DESTS) - 3 - filled], refs[len(refs) - 2 * len(DESTS) - 3:]
    outs, stack, kept, out_sems = refs[:len(DESTS) + 1], refs[len(DESTS) + 1], refs[len(DESTS) + 2:-1], refs[-1]
    windows, _, bins, part = ins[1].shape
    far, m, base, _ = whereabouts()
    blocks = counts_ref.shape[0]
    scale = 1.0 / math.sqrt(windows)
    norm = 1.0 / math.sqrt(bins)

    def sum_up(group, at, where):
        need = sorted({spot for pair in group for spot in pair})
        edges = sorted({edge for s in need for _, start, stop in where[s] for edge in (start, stop)})

        def tile(kt, carry):
            top = pl.multiple_of(kt * ROWS, ROWS)
            rows = pl.ds(top, ROWS)
            sums = (jnp.zeros((ROWS, part), jnp.float32),) * (2 * len(group))
            for start, stop in zip(edges, edges[1:]):
                def window(w, sums, start=start):
                    real, imag = {}, {}
                    for s in need:
                        array, begin = [(a, start - first) for a, first, last in where[s] if first <= start < last][0]
                        real[s] = ins[array][begin + w, 0, rows, :].astype(jnp.float32)
                        imag[s] = ins[array][begin + w, 1, rows, :].astype(jnp.float32)
                    out = []
                    for n, (a, b) in enumerate(group):
                        out.append(sums[2 * n] + (real[a] * real[b] + imag[a] * imag[b]))
                        out.append(sums[2 * n + 1] + (imag[a] * real[b] - real[a] * imag[b]))
                    return tuple(out)

                sums = lax.fori_loop(0, stop - start, window, sums, unroll=math.gcd(stop - start, 8))
            for n in range(len(group)):
                lanes = pl.ds((at + n) * part, part)
                stack[rows, lanes] = (sums[2 * n] * scale).astype(jnp.bfloat16)
                stack[pl.ds(pl.multiple_of(bins + top, ROWS), ROWS), lanes] = (sums[2 * n + 1] * scale).astype(jnp.bfloat16)
            return carry

        lax.fori_loop(0, bins // ROWS, tile, 0)

    for mine in range(2):
        @pl.when(m == mine)
        def _(mine=mine):
            copies = []
            for g, group in enumerate(work[mine]):
                at = len(flat(work[mine][:g]))
                sum_up(group, at, sources[mine])
                lags = jnp.dot(table_ref[far], stack[:, at * part:(at + len(group)) * part], preferred_element_type=jnp.float32)
                for n, (a, b) in enumerate(group):
                    first = jnp.where(far == 0, base + a, base + 3 - b)
                    reach = counts_ref[jnp.clip(first, 0, blocks - 1)]
                    corr = lags[:, n * part:(n + 1) * part] * jnp.where(reach >= b - a, norm, 0.0)
                    for spot, kind, rows in ((a, "ahead", corr[:bins]), (b, "back", corr[bins:])):
                        d, i = PLACE[spot]
                        row = items(spot).index((kind, b - a - 1))
                        kept[d][i, row] = rows.astype(jnp.bfloat16)
                        target = outs[d].at[row] if i == mine else outs[-1].at[STARTS[d] + row]
                        one = pltpu.make_async_copy(kept[d].at[i, row], target, out_sems.at[len(copies)])
                        one.start()
                        copies.append(one)
            for one in copies:
                one.wait()


def correlate(counts, tables, whites, work, sources, filled=(), weight=1):
    windows, _, bins, part = whites[1].shape
    most = max(len(flat(groups)) for groups in work)
    anywhere = pl.BlockSpec(memory_space=pl.ANY)
    scalars = pl.BlockSpec(memory_space=pltpu.SMEM)
    lengths = [size * (2 if d in MERGED else 1) for d, size in enumerate(SIZES)] + [sum(SIZES)]
    return pl.pallas_call(
        functools.partial(correlate_body, work=work, sources=sources, filled=len(filled)),
        in_specs=[scalars] + [pl.BlockSpec(memory_space=pltpu.VMEM)] * (1 + len(whites)) + [anywhere] * len(filled),
        out_specs=[anywhere] * len(lengths),
        out_shape=[jax.ShapeDtypeStruct((n, bins, part), jnp.bfloat16) for n in lengths],
        scratch_shapes=[
            pltpu.VMEM((2 * bins, most * part), jnp.bfloat16),
            *[pltpu.VMEM((2, size, bins, part), jnp.bfloat16) for size in SIZES],
            pltpu.SemaphoreType.DMA((2 * most,)),
        ],
        input_output_aliases={2 + len(whites) + i: i for i in range(len(filled))},
        compiler_params=pltpu.CompilerParams(vmem_limit_bytes=12 * MIB),
        cost_estimate=pl.CostEstimate(flops=weight * 100 * most * windows * bins * part, bytes_accessed=min(weight, 1) * 4 * len(whites) * windows * bins * part, transcendentals=0),
    )(counts, tables, *whites, *filled)


def merge_body(sib, *refs):
    outs, sems = refs[len(MERGED):-1], refs[-1]
    copies = []
    for n, d in enumerate(MERGED):
        copies.append(pltpu.make_async_copy(
            sib.at[pl.ds(STARTS[d], SIZES[d])], outs[n].at[pl.ds(SIZES[d], SIZES[d])], sems.at[n]))
    for one in copies:
        one.start()
    for one in copies:
        one.wait()


def merge(sib, own):
    anywhere = pl.BlockSpec(memory_space=pl.ANY)
    return pl.pallas_call(
        merge_body,
        in_specs=[pl.BlockSpec(memory_space=pltpu.VMEM)] + [anywhere] * len(own),
        out_specs=[anywhere] * len(own),
        out_shape=[jax.ShapeDtypeStruct(value.shape, value.dtype) for value in own],
        scratch_shapes=[pltpu.SemaphoreType.DMA((len(own),))],
        input_output_aliases={1 + i: i for i in range(len(own))},
        compiler_params=pltpu.CompilerParams(vmem_limit_bytes=4 * MIB),
    )(sib, *own)


def assemble_body(*refs, plan, count, filled):
    ins, refs = refs[:count], refs[count + 2 * filled:]
    forward, backward, wide, sems = refs
    far, m, _, q = whereabouts()
    part = ins[0].shape[2]
    for mine in range(2):
        @pl.when(m == mine)
        def _(mine=mine):
            waits = []
            for a, k, spot, first in plan[mine]:
                lanes = pl.ds(pl.multiple_of((q ^ k) * part, part), part)
                ahead = far if k < 2 else 1 - far
                for n, (kind, j) in enumerate(items(spot)):
                    at = len(waits)
                    wide[at] = ins[a][first + n].astype(jnp.float32)
                    side = ahead if kind == "ahead" else 1 - ahead
                    copies = [pltpu.make_async_copy(wide.at[at], ref.at[0, j, :, lanes], sems.at[at]) for ref in (forward, backward)]
                    for value, copy in enumerate(copies):
                        pl.when(side == value)(copy.start)
                    waits.append(copies[0])
            for copy in waits:
                copy.wait()


def assemble(parts, shape, plan, filled=(), weight=1):
    steps = max(sum(len(items(spot)) for _, _, spot, _ in one) for one in plan)
    anywhere = pl.BlockSpec(memory_space=pl.ANY)
    bins, part = parts[0].shape[1:]
    return pl.pallas_call(
        functools.partial(assemble_body, plan=plan, count=len(parts), filled=len(filled) // 2),
        in_specs=[pl.BlockSpec(memory_space=pltpu.VMEM)] * len(parts) + [anywhere] * len(filled),
        out_specs=[anywhere] * 2,
        out_shape=[jax.ShapeDtypeStruct((1,) + shape, jnp.float32)] * 2,
        scratch_shapes=[pltpu.VMEM((steps, bins, part), jnp.float32), pltpu.SemaphoreType.DMA((steps,))],
        input_output_aliases={len(parts) + i: i for i in range(len(filled))},
        compiler_params=pltpu.CompilerParams(vmem_limit_bytes=12 * MIB),
        cost_estimate=pl.CostEstimate(flops=weight * steps * bins * part, bytes_accessed=6 * steps * bins * part, transcendentals=0),
    )(*parts, *filled)


HERE = (0, 0, 0, 0)
OUTWARD = (-1, -1, 1, 1)
INWARD = (1, 1, -1, -1)
INNER_HERE = (None, 0, 0, None)
INNER_INWARD = (None, 1, -1, None)
INNER_OUTWARD = (None, -1, 1, None)


def send(value, flip, step):
    peers = lax.axis_size("chan")
    pairs = []
    for i in range(peers):
        planes = step[i % PLANE]
        if planes is not None and 0 <= i + PLANE * planes < peers:
            pairs.append((i, (i ^ flip) + PLANE * planes))
    return lax.ppermute(value, "chan", pairs)


def after(value, *done):
    return lax.optimization_barrier((value,) + done)[0]


def local(traces, mask, counts):
    _, windows, lags, width = traces.shape
    causal, tables = lag_tables(lags)
    tables = jnp.asarray(tables)
    rows = jnp.asarray(np.ascontiguousarray(causal.T))
    t2, t3 = whiten(mask, rows, traces, (windows, windows))
    t01, t1 = whiten(after(mask, t2), rows, traces, (2 * windows, windows))

    y2, y3 = send(t2, 2, HERE), send(t3, 3, HERE)
    z, e = send(t01, 0, OUTWARD), send(t01, 0, INNER_INWARD)
    u1 = send(t1, 1, HERE)
    r2 = send(after(y2, u1), 0, INWARD)
    r3b = send(after(t3, y2)[relayed(windows):], 3, OUTWARD)

    whole = lambda *arrays: {spot: ((array, 0, windows),) for spot, array in arrays}
    parts = correlate(
        counts, tables, (t01, u1, y2), ((NEAR[0],), (NEAR[1],)), sources=(
            whole((0, 0), (1, 1), (2, 2)),
            whole((0, 1), (1, 0), (3, 2))), weight=200)
    r3a = send(after(y3, parts[4])[:relayed(windows)], 0, INWARD)
    e1 = send(after(e, parts[4])[windows:], 1, INNER_HERE)
    parts = correlate(
        counts, tables, (t01, u1, y2, y3), ((REST[0],), (REST[1],)), sources=(
            whole((0, 0), (1, 1), (2, 2), (3, 3)),
            whole((0, 1), (1, 0), (2, 3), (3, 2))), filled=parts, weight=200)
    half = windows // 2
    z = after(z, parts[4])
    z1a, z1b = send(z[windows:windows + half], 1, HERE), send(z[windows + half:], 1, HERE)
    other = ((5, 0, half), (6, half, windows))
    parts = correlate(
        counts, tables, (t01, u1, y2, y3, z, z1a, z1b, r2, e1, e), ((BEYOND, INNER, FIRST), (BEYOND, OUTER, FIRST)), sources=(
            whole((0, 0), (1, 1), (2, 2), (3, 3), (4, 4), (-2, 7), (-3, 8)) | {5: other},
            whole((0, 1), (1, 0), (2, 3), (3, 2), (5, 4), (-1, 7), (-3, 9)) | {4: other}), filled=parts, weight=0)
    last = ((5, 0, relayed(windows)), (6, relayed(windows), windows))
    keep, f, x, v, w, sib = correlate(
        counts, tables, (t01, u1, y2, y3, z, r3a, r3b), ((OUTER,), (INNER,)), sources=(
            whole((0, 0), (1, 1), (2, 2), (3, 3), (4, 4)) | {-1: last},
            whole((0, 1), (1, 0), (2, 3), (3, 2)) | {-2: last}), filled=parts)

    near = send(f, 2, HERE)
    sib = send(sib, 1, HERE)
    x, v, w = merge(sib, (x, v, w))
    rest = send(sib[STARTS[1]:STARTS[2]], 2, HERE)
    v, x = send(v, 2, OUTWARD), send(x, 0, INWARD)
    w = send(w, 0, INNER_OUTWARD)

    shape = (MAXP, lags // 2, width)
    filled = assemble((keep, sib), shape, [[(0, 0, mine, 0), (1, 1, mine, 0)] for mine in range(2)])
    filled = assemble((near,), shape, [[(0, 2, 3 - mine, 0)] for mine in range(2)], filled, weight=50000)
    return tuple(assemble((rest, x, v, w), shape, [
        [(0, 3, 3 - mine, 0), (1, 0, 4 + mine, 0), (1, 1, 4 + mine, SIZES[2]),
         (2, 2, -1 - mine, 0), (2, 3, -1 - mine, SIZES[3])] + inner
        for mine, inner in enumerate(([], [(3, 0, -3, 0), (3, 1, -3, 1)]))], filled))


def solution(mesh):
    return jax.shard_map(
        local,
        mesh=mesh,
        in_specs=(P(("grp", "chan"), None, None, None), P("grp", None), P("grp")),
        out_specs=(P(("grp", "chan"), None, None, None), P(("grp", "chan"), None, None, None)),
        check_vma=False,
    )
```

```python
import functools
import math

import jax
import jax.numpy as jnp
import numpy as np
from jax import lax
from jax.experimental import pallas as pl
from jax.experimental.pallas import tpu as pltpu
from jax.sharding import PartitionSpec as P

MAXP = 5
PLANE = 4
MIB = 1024 * 1024
ROWS = 16
STEP = 8

NEAR = (((0, 1), (0, 2), (1, 2)), ((0, 1), (0, 3), (1, 3)))
REST = (((0, 3), (1, 3), (2, 3)), ((0, 2), (1, 2), (2, 3)))
FIRST = ((-3, 2),)
BEYOND = ((0, 4), (0, 5), (1, 4), (1, 5), (3, 5))
OUTER = ((-1, 0), (-1, 2), (-1, 3), (-1, 4))
INNER = ((-2, 0), (-2, 1), (-2, 2), (-2, 3))
PAIRS = NEAR[0] + REST[0] + FIRST + BEYOND + OUTER + INNER
DESTS = ((0, 1), (2, 3), (4, 5), (-2, -1), (None, -3))


def flat(groups):
    return [pair for group in groups for pair in group]


def items(spot):
    ahead = sorted(("ahead", b - a - 1) for a, b in PAIRS if a == spot)
    back = sorted(("back", b - a - 1) for a, b in PAIRS if b == spot)
    return ahead + back


MERGED = (2, 3, 4)
SIZES = [max(len(items(spot)) for spot in spots) for spots in DESTS]
STARTS = [sum(SIZES[:d]) for d in range(len(SIZES))]
PLACE = {spot: (d, i) for d, spots in enumerate(DESTS) for i, spot in enumerate(spots)}


def lag_tables(lags):
    bins = lags // 2
    phase = (np.arange(lags)[:, None] * np.arange(1, bins + 1)[None, :] % lags) * (2.0 * math.pi / lags)
    real, imag = np.cos(phase), -np.sin(phase)
    causal = np.concatenate([real, imag], axis=1)
    other = np.concatenate([real, -imag], axis=1)
    near = np.concatenate([causal[:bins], causal[bins:][::-1]], axis=0)
    far = np.concatenate([other[bins:][::-1], other[:bins]], axis=0)
    return causal.astype(jnp.bfloat16), np.stack([near, far]).astype(jnp.bfloat16)


def whereabouts():
    me = lax.axis_index("chan").astype(jnp.int32)
    q = lax.rem(me, PLANE)
    far = q // 2
    return far, lax.rem(q, 2) ^ far, me - q, q


def whiten_body(mask_ref, table_ref, traces_ref, *refs):
    outs, (white, sems) = refs[:-2], refs[-2:]
    _, _, base, q = whereabouts()
    windows = white.shape[1]
    bins = table_ref.shape[0] // 2
    part = white.shape[-1]
    step = traces_ref.shape[1]
    at = pl.program_id(0)
    for n in range(step):
        w = at * step + n
        raw = jnp.dot(table_ref[...], traces_ref[0, n], preferred_element_type=jnp.float32)
        power = jnp.sum(raw * raw, axis=0, keepdims=True) / bins
        valid = mask_ref[base + q, w].astype(jnp.float32)
        scaled = (raw * (valid * lax.rsqrt(power + 1e-06))).astype(jnp.bfloat16)
        for quarter in range(2):
            piece = scaled[:, quarter * part:(quarter + 1) * part]
            white[quarter ^ lax.rem(q, 2), w, 0] = piece[:bins]
            white[quarter ^ lax.rem(q, 2), w, 1] = piece[bins:]

    def copies(i):
        span = pl.ds(i * step, step)
        targets = [(n, out.at[span]) for n, out in enumerate(outs)]
        if outs[0].shape[0] > windows:
            targets.append((1, outs[0].at[pl.ds(windows + i * step, step)]))
        return [pltpu.make_async_copy(white.at[k, span], target, sems.at[n, i]) for n, (k, target) in enumerate(targets)]

    for one in copies(at):
        one.start()

    @pl.when(at == pl.num_programs(0) - 1)
    def _():
        for i in range(sems.shape[1]):
            for one in copies(i):
                one.wait()


def whiten(mask, table, traces, lengths):
    _, windows, lags, width = traces.shape
    bins = lags // 2
    part = width // PLANE
    other = lengths[0] == windows

    def half(i):
        far = whereabouts()[0]
        return 0, i, 0, 1 - far if other else far

    return pl.pallas_call(
        whiten_body,
        grid=(windows // STEP,),
        in_specs=[
            pl.BlockSpec(memory_space=pltpu.SMEM),
            pl.BlockSpec((lags, lags), lambda i: (0, 0)),
            pl.BlockSpec((1, STEP, lags, 2 * part), half),
        ],
        out_specs=[pl.BlockSpec(memory_space=pl.ANY)] * len(lengths),
        out_shape=[jax.ShapeDtypeStruct((n, 2, bins, part), jnp.bfloat16) for n in lengths],
        scratch_shapes=[
            pltpu.VMEM((2, windows, 2, bins, part), jnp.bfloat16),
            pltpu.SemaphoreType.DMA((3, windows // STEP)),
        ],
        compiler_params=pltpu.CompilerParams(vmem_limit_bytes=57 * MIB),
        cost_estimate=pl.CostEstimate(flops=windows * lags * lags * width, bytes_accessed=2 * windows * lags * width, transcendentals=0),
    )(mask, table, traces)


def relayed(windows):
    return windows * 11 // 16


def correlate_body(counts_ref, table_ref, *refs, work, sources, filled):
    count = len(DESTS) + 1
    outs, stack = refs[-count - 1:-1], refs[-1]
    held, ins = refs[len(refs) - count - 1 - filled:-count - 1], refs[:len(refs) - count - 1 - filled]
    windows, _, bins, part = ins[1].shape
    far, m, base, _ = whereabouts()
    blocks = counts_ref.shape[0]
    scale = 1.0 / math.sqrt(windows)
    norm = 1.0 / math.sqrt(bins)

    def sum_up(group, at, where):
        need = sorted({spot for pair in group for spot in pair})
        edges = sorted({edge for s in need for _, start, stop in where[s] for edge in (start, stop)})

        def tile(kt, carry):
            top = pl.multiple_of(kt * ROWS, ROWS)
            rows = pl.ds(top, ROWS)
            sums = (jnp.zeros((ROWS, part), jnp.float32),) * (2 * len(group))
            for start, stop in zip(edges, edges[1:]):
                def window(w, sums, start=start):
                    real, imag = {}, {}
                    for s in need:
                        array, begin = [(a, start - first) for a, first, last in where[s] if first <= start < last][0]
                        real[s] = ins[array][begin + w, 0, rows, :].astype(jnp.float32)
                        imag[s] = ins[array][begin + w, 1, rows, :].astype(jnp.float32)
                    out = []
                    for n, (a, b) in enumerate(group):
                        out.append(sums[2 * n] + (real[a] * real[b] + imag[a] * imag[b]))
                        out.append(sums[2 * n + 1] + (imag[a] * real[b] - real[a] * imag[b]))
                    return tuple(out)

                sums = lax.fori_loop(0, stop - start, window, sums, unroll=stop - start if stop - start <= 12 else 8)
            for n in range(len(group)):
                lanes = pl.ds((at + n) * part, part)
                stack[rows, lanes] = (sums[2 * n] * scale).astype(jnp.bfloat16)
                stack[pl.ds(pl.multiple_of(bins + top, ROWS), ROWS), lanes] = (sums[2 * n + 1] * scale).astype(jnp.bfloat16)
            return carry

        lax.fori_loop(0, bins // ROWS, tile, 0)

    for mine in range(2):
        @pl.when(m == mine)
        def _(mine=mine):
            for out, old in zip(outs, held):
                out[...] = old[...]
            for g, group in enumerate(work[mine]):
                at = len(flat(work[mine][:g]))
                sum_up(group, at, sources[mine])
                lags = jnp.dot(table_ref[far], stack[:, at * part:(at + len(group)) * part], preferred_element_type=jnp.float32)
                for n, (a, b) in enumerate(group):
                    first = jnp.where(far == 0, base + a, base + 3 - b)
                    reach = counts_ref[jnp.clip(first, 0, blocks - 1)]
                    corr = lags[:, n * part:(n + 1) * part] * jnp.where(reach >= b - a, norm, 0.0)
                    for spot, kind, rows in ((a, "ahead", corr[:bins]), (b, "back", corr[bins:])):
                        d, i = PLACE[spot]
                        row = items(spot).index((kind, b - a - 1))
                        out, row = (outs[d], row) if i == mine else (outs[-1], STARTS[d] + row)
                        out[row] = rows.astype(jnp.bfloat16)


def correlate(counts, tables, whites, work, sources, filled=(), weight=1):
    windows, _, bins, part = whites[1].shape
    most = max(len(flat(groups)) for groups in work)
    scalars = pl.BlockSpec(memory_space=pltpu.SMEM)
    lengths = [size * (2 if d in MERGED else 1) for d, size in enumerate(SIZES)] + [sum(SIZES)]
    return pl.pallas_call(
        functools.partial(correlate_body, work=work, sources=sources, filled=len(filled)),
        in_specs=[scalars] + [pl.BlockSpec(memory_space=pltpu.VMEM)] * (1 + len(whites) + len(filled)),
        out_specs=[pl.BlockSpec(memory_space=pltpu.VMEM)] * len(lengths),
        out_shape=[jax.ShapeDtypeStruct((n, bins, part), jnp.bfloat16) for n in lengths],
        scratch_shapes=[pltpu.VMEM((2 * bins, most * part), jnp.bfloat16)],
        compiler_params=pltpu.CompilerParams(vmem_limit_bytes=12 * MIB),
        cost_estimate=pl.CostEstimate(flops=weight * 100 * most * windows * bins * part, bytes_accessed=min(weight, 1) * 4 * len(whites) * windows * bins * part, transcendentals=0),
    )(counts, tables, *whites, *filled)


def merge_body(sib, *refs):
    outs, sems = refs[len(MERGED):-1], refs[-1]
    copies = []
    for n, d in enumerate(MERGED):
        copies.append(pltpu.make_async_copy(
            sib.at[pl.ds(STARTS[d], SIZES[d])], outs[n].at[pl.ds(SIZES[d], SIZES[d])], sems.at[n]))
    for one in copies:
        one.start()
    for one in copies:
        one.wait()


def merge(sib, own):
    anywhere = pl.BlockSpec(memory_space=pl.ANY)
    return pl.pallas_call(
        merge_body,
        in_specs=[pl.BlockSpec(memory_space=pltpu.VMEM)] + [anywhere] * len(own),
        out_specs=[anywhere] * len(own),
        out_shape=[jax.ShapeDtypeStruct(value.shape, value.dtype) for value in own],
        scratch_shapes=[pltpu.SemaphoreType.DMA((len(own),))],
        input_output_aliases={1 + i: i for i in range(len(own))},
        compiler_params=pltpu.CompilerParams(vmem_limit_bytes=4 * MIB),
    )(sib, *own)


def assemble_body(*refs, plan, count, filled):
    ins, refs = refs[:count], refs[count + 2 * filled:]
    forward, backward, wide, sems = refs
    far, m, _, q = whereabouts()
    part = ins[0].shape[2]
    for mine in range(2):
        @pl.when(m == mine)
        def _(mine=mine):
            waits = []
            for a, k, spot, first in plan[mine]:
                lanes = pl.ds(pl.multiple_of((q ^ k) * part, part), part)
                ahead = far if k < 2 else 1 - far
                for n, (kind, j) in enumerate(items(spot)):
                    at = len(waits)
                    wide[at] = ins[a][first + n].astype(jnp.float32)
                    side = ahead if kind == "ahead" else 1 - ahead
                    copies = [pltpu.make_async_copy(wide.at[at], ref.at[0, j, :, lanes], sems.at[at]) for ref in (forward, backward)]
                    for value, copy in enumerate(copies):
                        pl.when(side == value)(copy.start)
                    waits.append(copies[0])
            for copy in waits:
                copy.wait()


def assemble(parts, shape, plan, filled=(), weight=1):
    steps = max(sum(len(items(spot)) for _, _, spot, _ in one) for one in plan)
    anywhere = pl.BlockSpec(memory_space=pl.ANY)
    bins, part = parts[0].shape[1:]
    return pl.pallas_call(
        functools.partial(assemble_body, plan=plan, count=len(parts), filled=len(filled) // 2),
        in_specs=[pl.BlockSpec(memory_space=pltpu.VMEM)] * len(parts) + [anywhere] * len(filled),
        out_specs=[anywhere] * 2,
        out_shape=[jax.ShapeDtypeStruct((1,) + shape, jnp.float32)] * 2,
        scratch_shapes=[pltpu.VMEM((steps, bins, part), jnp.float32), pltpu.SemaphoreType.DMA((steps,))],
        input_output_aliases={len(parts) + i: i for i in range(len(filled))},
        compiler_params=pltpu.CompilerParams(vmem_limit_bytes=12 * MIB),
        cost_estimate=pl.CostEstimate(flops=weight * steps * bins * part, bytes_accessed=6 * steps * bins * part, transcendentals=0),
    )(*parts, *filled)


HERE = (0, 0, 0, 0)
OUTWARD = (-1, -1, 1, 1)
INWARD = (1, 1, -1, -1)
INNER_HERE = (None, 0, 0, None)
INNER_INWARD = (None, 1, -1, None)
INNER_OUTWARD = (None, -1, 1, None)


def send(value, flip, step):
    peers = lax.axis_size("chan")
    pairs = []
    for i in range(peers):
        planes = step[i % PLANE]
        if planes is not None and 0 <= i + PLANE * planes < peers:
            pairs.append((i, (i ^ flip) + PLANE * planes))
    return lax.ppermute(value, "chan", pairs)


def after(value, *done):
    return lax.optimization_barrier((value,) + done)[0]


def local(traces, mask, counts):
    _, windows, lags, width = traces.shape
    causal, tables = lag_tables(lags)
    tables = jnp.asarray(tables)
    rows = jnp.asarray(np.ascontiguousarray(causal.T))
    t2, t3 = whiten(mask, rows, traces, (windows, windows))
    t01, t1 = whiten(after(mask, t2), rows, traces, (2 * windows, windows))

    y2, y3 = send(t2, 2, HERE), send(t3, 3, HERE)
    z, e = send(t01, 0, OUTWARD), send(t01, 0, INNER_INWARD)
    u1 = send(t1, 1, HERE)
    r2 = send(after(y2, u1), 0, INWARD)
    r3b = send(after(t3, y2)[relayed(windows):], 3, OUTWARD)

    whole = lambda *arrays: {spot: ((array, 0, windows),) for spot, array in arrays}
    parts = correlate(
        counts, tables, (t01, u1, y2), ((NEAR[0],), (NEAR[1],)), sources=(
            whole((0, 0), (1, 1), (2, 2)),
            whole((0, 1), (1, 0), (3, 2))), weight=200)
    r3a = send(after(y3, parts[4])[:relayed(windows)], 0, INWARD)
    e1 = send(after(e, parts[4])[windows:], 1, INNER_HERE)
    parts = correlate(
        counts, tables, (t01, u1, y2, y3), ((REST[0],), (REST[1],)), sources=(
            whole((0, 0), (1, 1), (2, 2), (3, 3)),
            whole((0, 1), (1, 0), (2, 3), (3, 2))), filled=parts, weight=200)
    half = windows // 2
    z = after(z, parts[4])
    z1a, z1b = send(z[windows:windows + half], 1, HERE), send(z[windows + half:], 1, HERE)
    other = ((5, 0, half), (6, half, windows))
    parts = correlate(
        counts, tables, (t01, u1, y2, y3, z, z1a, z1b, r2, e1, e), ((BEYOND, INNER, FIRST), (BEYOND, OUTER, FIRST)), sources=(
            whole((0, 0), (1, 1), (2, 2), (3, 3), (4, 4), (-2, 7), (-3, 8)) | {5: other},
            whole((0, 1), (1, 0), (2, 3), (3, 2), (5, 4), (-1, 7), (-3, 9)) | {4: other}), filled=parts, weight=0)
    last = ((5, 0, relayed(windows)), (6, relayed(windows), windows))
    keep, f, x, v, w, sib = correlate(
        counts, tables, (t01, u1, y2, y3, z, r3a, r3b), ((OUTER,), (INNER,)), sources=(
            whole((0, 0), (1, 1), (2, 2), (3, 3), (4, 4)) | {-1: last},
            whole((0, 1), (1, 0), (2, 3), (3, 2)) | {-2: last}), filled=parts)

    near = send(f, 2, HERE)
    sib = send(sib, 1, HERE)
    x, v, w = merge(sib, (x, v, w))
    rest = send(sib[STARTS[1]:STARTS[2]], 2, HERE)
    v, x = send(v, 2, OUTWARD), send(x, 0, INWARD)
    w = send(w, 0, INNER_OUTWARD)

    shape = (MAXP, lags // 2, width)
    filled = assemble((keep, sib), shape, [[(0, 0, mine, 0), (1, 1, mine, 0)] for mine in range(2)])
    filled = assemble((near,), shape, [[(0, 2, 3 - mine, 0)] for mine in range(2)], filled, weight=12000)
    return tuple(assemble((rest, x, v, w), shape, [
        [(0, 3, 3 - mine, 0), (1, 0, 4 + mine, 0), (1, 1, 4 + mine, SIZES[2]),
         (2, 2, -1 - mine, 0), (2, 3, -1 - mine, SIZES[3])] + inner
        for mine, inner in enumerate(([], [(3, 0, -3, 0), (3, 1, -3, 1)]))], filled))


def solution(mesh):
    return jax.shard_map(
        local,
        mesh=mesh,
        in_specs=(P(("grp", "chan"), None, None, None), P("grp", None), P("grp")),
        out_specs=(P(("grp", "chan"), None, None, None), P(("grp", "chan"), None, None, None)),
        check_vma=False,
    )
```

```python
import functools
import math

import jax
import jax.numpy as jnp
import numpy as np
from jax import lax
from jax.experimental import pallas as pl
from jax.experimental.pallas import tpu as pltpu
from jax.sharding import PartitionSpec as P

MAXP = 5
PLANE = 4
MIB = 1024 * 1024
ROWS = 16
STEP = 8

NEAR = (((0, 1), (0, 2), (1, 2)), ((0, 1), (0, 3), (1, 3)))
REST = (((0, 3), (1, 3), (2, 3)), ((0, 2), (1, 2), (2, 3)))
FIRST = ((-3, 2),)
BEYOND = ((0, 4), (0, 5), (1, 4), (1, 5), (3, 5))
OUTER = ((-1, 0), (-1, 2), (-1, 3), (-1, 4))
INNER = ((-2, 0), (-2, 1), (-2, 2), (-2, 3))
PAIRS = NEAR[0] + REST[0] + FIRST + BEYOND + OUTER + INNER
DESTS = ((0, 1), (2, 3), (4, 5), (-2, -1), (None, -3))


def flat(groups):
    return [pair for group in groups for pair in group]


def items(spot):
    ahead = sorted(("ahead", b - a - 1) for a, b in PAIRS if a == spot)
    back = sorted(("back", b - a - 1) for a, b in PAIRS if b == spot)
    return ahead + back


MERGED = (2, 3, 4)
SIZES = [max(len(items(spot)) for spot in spots) for spots in DESTS]
STARTS = [sum(SIZES[:d]) for d in range(len(SIZES))]
PLACE = {spot: (d, i) for d, spots in enumerate(DESTS) for i, spot in enumerate(spots)}


def lag_tables(lags):
    bins = lags // 2
    phase = (np.arange(lags)[:, None] * np.arange(1, bins + 1)[None, :] % lags) * (2.0 * math.pi / lags)
    real, imag = np.cos(phase), -np.sin(phase)
    causal = np.concatenate([real, imag], axis=1)
    other = np.concatenate([real, -imag], axis=1)
    near = np.concatenate([causal[:bins], causal[bins:][::-1]], axis=0)
    far = np.concatenate([other[bins:][::-1], other[:bins]], axis=0)
    return causal.astype(jnp.bfloat16), np.stack([near, far]).astype(jnp.bfloat16)


def whereabouts():
    me = lax.axis_index("chan").astype(jnp.int32)
    q = lax.rem(me, PLANE)
    far = q // 2
    return far, lax.rem(q, 2) ^ far, me - q, q


def whiten_body(mask_ref, table_ref, traces_ref, *refs):
    outs, (white, sems) = refs[:-2], refs[-2:]
    _, _, base, q = whereabouts()
    windows = white.shape[1]
    bins = table_ref.shape[0] // 2
    part = white.shape[-1]
    step = traces_ref.shape[1]
    at = pl.program_id(0)
    for n in range(step):
        w = at * step + n
        raw = jnp.dot(table_ref[...], traces_ref[0, n], preferred_element_type=jnp.float32)
        power = jnp.sum(raw * raw, axis=0, keepdims=True) / bins
        valid = mask_ref[base + q, w].astype(jnp.float32)
        scaled = (raw * (valid * lax.rsqrt(power + 1e-06))).astype(jnp.bfloat16)
        for quarter in range(2):
            piece = scaled[:, quarter * part:(quarter + 1) * part]
            white[quarter ^ lax.rem(q, 2), w, 0] = piece[:bins]
            white[quarter ^ lax.rem(q, 2), w, 1] = piece[bins:]

    def copies(i):
        span = pl.ds(i * step, step)
        targets = [(n, out.at[span]) for n, out in enumerate(outs)]
        if outs[0].shape[0] > windows:
            targets.append((1, outs[0].at[pl.ds(windows + i * step, step)]))
        return [pltpu.make_async_copy(white.at[k, span], target, sems.at[n, i]) for n, (k, target) in enumerate(targets)]

    for one in copies(at):
        one.start()

    @pl.when(at == pl.num_programs(0) - 1)
    def _():
        for i in range(sems.shape[1]):
            for one in copies(i):
                one.wait()


def whiten(mask, table, traces, lengths):
    _, windows, lags, width = traces.shape
    bins = lags // 2
    part = width // PLANE
    other = lengths[0] == windows

    def half(i):
        far = whereabouts()[0]
        return 0, i, 0, 1 - far if other else far

    return pl.pallas_call(
        whiten_body,
        grid=(windows // STEP,),
        in_specs=[
            pl.BlockSpec(memory_space=pltpu.SMEM),
            pl.BlockSpec((lags, lags), lambda i: (0, 0)),
            pl.BlockSpec((1, STEP, lags, 2 * part), half),
        ],
        out_specs=[pl.BlockSpec(memory_space=pl.ANY)] * len(lengths),
        out_shape=[jax.ShapeDtypeStruct((n, 2, bins, part), jnp.bfloat16) for n in lengths],
        scratch_shapes=[
            pltpu.VMEM((2, windows, 2, bins, part), jnp.bfloat16),
            pltpu.SemaphoreType.DMA((3, windows // STEP)),
        ],
        compiler_params=pltpu.CompilerParams(vmem_limit_bytes=57 * MIB),
        cost_estimate=pl.CostEstimate(flops=windows * lags * lags * width, bytes_accessed=2 * windows * lags * width, transcendentals=0),
    )(mask, table, traces)


def relayed(windows):
    return windows * 11 // 16


def correlate_body(counts_ref, table_ref, *refs, work, sources, filled):
    count = len(DESTS) + 1
    outs, stack = refs[-count - 1:-1], refs[-1]
    held, ins = refs[len(refs) - count - 1 - filled:-count - 1], refs[:len(refs) - count - 1 - filled]
    windows, _, bins, part = ins[1].shape
    far, m, base, _ = whereabouts()
    blocks = counts_ref.shape[0]
    scale = 1.0 / math.sqrt(windows)
    norm = 1.0 / math.sqrt(bins)

    def sum_up(group, at, where):
        need = sorted({spot for pair in group for spot in pair})
        edges = sorted({edge for s in need for _, start, stop in where[s] for edge in (start, stop)})

        def tile(kt, carry):
            top = pl.multiple_of(kt * ROWS, ROWS)
            rows = pl.ds(top, ROWS)
            sums = (jnp.zeros((ROWS, part), jnp.float32),) * (2 * len(group))
            for start, stop in zip(edges, edges[1:]):
                def window(w, sums, start=start):
                    real, imag = {}, {}
                    for s in need:
                        array, begin = [(a, start - first) for a, first, last in where[s] if first <= start < last][0]
                        real[s] = ins[array][begin + w, 0, rows, :].astype(jnp.float32)
                        imag[s] = ins[array][begin + w, 1, rows, :].astype(jnp.float32)
                    out = []
                    for n, (a, b) in enumerate(group):
                        out.append(sums[2 * n] + (real[a] * real[b] + imag[a] * imag[b]))
                        out.append(sums[2 * n + 1] + (imag[a] * real[b] - real[a] * imag[b]))
                    return tuple(out)

                sums = lax.fori_loop(0, stop - start, window, sums, unroll=stop - start if stop - start <= 12 else 8)
            for n in range(len(group)):
                lanes = pl.ds((at + n) * part, part)
                stack[rows, lanes] = (sums[2 * n] * scale).astype(jnp.bfloat16)
                stack[pl.ds(pl.multiple_of(bins + top, ROWS), ROWS), lanes] = (sums[2 * n + 1] * scale).astype(jnp.bfloat16)
            return carry

        lax.fori_loop(0, bins // ROWS, tile, 0)

    for mine in range(2):
        @pl.when(m == mine)
        def _(mine=mine):
            for out, old in zip(outs, held):
                out[...] = old[...]
            for g, group in enumerate(work[mine]):
                at = len(flat(work[mine][:g]))
                sum_up(group, at, sources[mine])
                lags = jnp.dot(table_ref[far], stack[:, at * part:(at + len(group)) * part], preferred_element_type=jnp.float32)
                for n, (a, b) in enumerate(group):
                    first = jnp.where(far == 0, base + a, base + 3 - b)
                    reach = counts_ref[jnp.clip(first, 0, blocks - 1)]
                    corr = lags[:, n * part:(n + 1) * part] * jnp.where(reach >= b - a, norm, 0.0)
                    for spot, kind, rows in ((a, "ahead", corr[:bins]), (b, "back", corr[bins:])):
                        d, i = PLACE[spot]
                        row = items(spot).index((kind, b - a - 1))
                        out, row = (outs[d], row) if i == mine else (outs[-1], STARTS[d] + row)
                        out[row] = rows.astype(jnp.bfloat16)


def correlate(counts, tables, whites, work, sources, filled=(), weight=1):
    windows, _, bins, part = whites[1].shape
    most = max(len(flat(groups)) for groups in work)
    scalars = pl.BlockSpec(memory_space=pltpu.SMEM)
    lengths = [size * (2 if d in MERGED else 1) for d, size in enumerate(SIZES)] + [sum(SIZES)]
    return pl.pallas_call(
        functools.partial(correlate_body, work=work, sources=sources, filled=len(filled)),
        in_specs=[scalars] + [pl.BlockSpec(memory_space=pltpu.VMEM)] * (1 + len(whites) + len(filled)),
        out_specs=[pl.BlockSpec(memory_space=pltpu.VMEM)] * len(lengths),
        out_shape=[jax.ShapeDtypeStruct((n, bins, part), jnp.bfloat16) for n in lengths],
        scratch_shapes=[pltpu.VMEM((2 * bins, most * part), jnp.bfloat16)],
        compiler_params=pltpu.CompilerParams(vmem_limit_bytes=12 * MIB),
        cost_estimate=pl.CostEstimate(flops=weight * 100 * most * windows * bins * part, bytes_accessed=min(weight, 1) * 4 * len(whites) * windows * bins * part, transcendentals=0),
    )(counts, tables, *whites, *filled)


def merge_body(sib, *refs):
    outs, sems = refs[len(MERGED):-1], refs[-1]
    copies = []
    for n, d in enumerate(MERGED):
        copies.append(pltpu.make_async_copy(
            sib.at[pl.ds(STARTS[d], SIZES[d])], outs[n].at[pl.ds(SIZES[d], SIZES[d])], sems.at[n]))
    for one in copies:
        one.start()
    for one in copies:
        one.wait()


def merge(sib, own):
    anywhere = pl.BlockSpec(memory_space=pl.ANY)
    return pl.pallas_call(
        merge_body,
        in_specs=[pl.BlockSpec(memory_space=pltpu.VMEM)] + [anywhere] * len(own),
        out_specs=[anywhere] * len(own),
        out_shape=[jax.ShapeDtypeStruct(value.shape, value.dtype) for value in own],
        scratch_shapes=[pltpu.SemaphoreType.DMA((len(own),))],
        input_output_aliases={1 + i: i for i in range(len(own))},
        compiler_params=pltpu.CompilerParams(vmem_limit_bytes=4 * MIB),
    )(sib, *own)


def assemble_body(*refs, plan, count, filled):
    ins, refs = refs[:count], refs[count + 2 * filled:]
    forward, backward, wide, sems = refs
    far, m, _, q = whereabouts()
    part = ins[0].shape[2]
    for mine in range(2):
        @pl.when(m == mine)
        def _(mine=mine):
            waits = []
            for a, k, spot, first in plan[mine]:
                lanes = pl.ds(pl.multiple_of((q ^ k) * part, part), part)
                ahead = far if k < 2 else 1 - far
                for n, (kind, j) in enumerate(items(spot)):
                    at = len(waits)
                    wide[at] = ins[a][first + n].astype(jnp.float32)
                    side = ahead if kind == "ahead" else 1 - ahead
                    copies = [pltpu.make_async_copy(wide.at[at], ref.at[0, j, :, lanes], sems.at[at]) for ref in (forward, backward)]
                    for value, copy in enumerate(copies):
                        pl.when(side == value)(copy.start)
                    waits.append(copies[0])
            for copy in waits:
                copy.wait()


def assemble(parts, shape, plan, filled=(), weight=1):
    steps = max(sum(len(items(spot)) for _, _, spot, _ in one) for one in plan)
    anywhere = pl.BlockSpec(memory_space=pl.ANY)
    bins, part = parts[0].shape[1:]
    return pl.pallas_call(
        functools.partial(assemble_body, plan=plan, count=len(parts), filled=len(filled) // 2),
        in_specs=[pl.BlockSpec(memory_space=pltpu.VMEM)] * len(parts) + [anywhere] * len(filled),
        out_specs=[anywhere] * 2,
        out_shape=[jax.ShapeDtypeStruct((1,) + shape, jnp.float32)] * 2,
        scratch_shapes=[pltpu.VMEM((steps, bins, part), jnp.float32), pltpu.SemaphoreType.DMA((steps,))],
        input_output_aliases={len(parts) + i: i for i in range(len(filled))},
        compiler_params=pltpu.CompilerParams(vmem_limit_bytes=12 * MIB),
        cost_estimate=pl.CostEstimate(flops=weight * steps * bins * part, bytes_accessed=6 * steps * bins * part, transcendentals=0),
    )(*parts, *filled)


HERE = (0, 0, 0, 0)
OUTWARD = (-1, -1, 1, 1)
INWARD = (1, 1, -1, -1)
INNER_HERE = (None, 0, 0, None)
INNER_INWARD = (None, 1, -1, None)
INNER_OUTWARD = (None, -1, 1, None)


def send(value, flip, step):
    peers = lax.axis_size("chan")
    pairs = []
    for i in range(peers):
        planes = step[i % PLANE]
        if planes is not None and 0 <= i + PLANE * planes < peers:
            pairs.append((i, (i ^ flip) + PLANE * planes))
    return lax.ppermute(value, "chan", pairs)


def after(value, *done):
    return lax.optimization_barrier((value,) + done)[0]


def local(traces, mask, counts):
    _, windows, lags, width = traces.shape
    causal, tables = lag_tables(lags)
    tables = jnp.asarray(tables)
    rows = jnp.asarray(np.ascontiguousarray(causal.T))
    t2, t3 = whiten(mask, rows, traces, (windows, windows))
    t01, t1 = whiten(after(mask, t2), rows, traces, (2 * windows, windows))

    y2, y3 = send(t2, 2, HERE), send(t3, 3, HERE)
    z, e = send(t01, 0, OUTWARD), send(t01, 0, INNER_INWARD)
    u1 = send(t1, 1, HERE)
    r2 = send(after(y2, u1), 0, INWARD)
    r3b = send(after(t3, y2)[relayed(windows):], 3, OUTWARD)

    whole = lambda *arrays: {spot: ((array, 0, windows),) for spot, array in arrays}
    parts = correlate(
        counts, tables, (t01, u1, y2), ((NEAR[0],), (NEAR[1],)), sources=(
            whole((0, 0), (1, 1), (2, 2)),
            whole((0, 1), (1, 0), (3, 2))), weight=200)
    r3a = send(after(y3, parts[4])[:relayed(windows)], 0, INWARD)
    e1 = send(after(e, parts[4])[windows:], 1, INNER_HERE)
    parts = correlate(
        counts, tables, (t01, u1, y2, y3), ((REST[0],), (REST[1],)), sources=(
            whole((0, 0), (1, 1), (2, 2), (3, 3)),
            whole((0, 1), (1, 0), (2, 3), (3, 2))), filled=parts, weight=200)
    half = windows // 2
    z = after(z, parts[4])
    z1a, z1b = send(z[windows:windows + half], 1, HERE), send(z[windows + half:], 1, HERE)
    other = ((5, 0, half), (6, half, windows))
    parts = correlate(
        counts, tables, (t01, u1, y2, y3, z, z1a, z1b, r2, e1, e), ((BEYOND, INNER, FIRST), (BEYOND, OUTER, FIRST)), sources=(
            whole((0, 0), (1, 1), (2, 2), (3, 3), (4, 4), (-2, 7), (-3, 8)) | {5: other},
            whole((0, 1), (1, 0), (2, 3), (3, 2), (5, 4), (-1, 7), (-3, 9)) | {4: other}), filled=parts, weight=0)
    last = ((5, 0, relayed(windows)), (6, relayed(windows), windows))
    keep, f, x, v, w, sib = correlate(
        counts, tables, (t01, u1, y2, y3, z, r3a, r3b), ((OUTER,), (INNER,)), sources=(
            whole((0, 0), (1, 1), (2, 2), (3, 3), (4, 4)) | {-1: last},
            whole((0, 1), (1, 0), (2, 3), (3, 2)) | {-2: last}), filled=parts)

    near = send(f, 2, HERE)
    sib = send(sib, 1, HERE)
    x, v, w = merge(sib, (x, v, w))
    rest = send(sib[STARTS[1]:STARTS[2]], 2, HERE)
    v, x = send(v, 2, OUTWARD), send(x, 0, INWARD)
    w = send(w, 0, INNER_OUTWARD)

    shape = (MAXP, lags // 2, width)
    filled = assemble((keep, sib), shape, [[(0, 0, mine, 0), (1, 1, mine, 0)] for mine in range(2)])
    filled = assemble((near,), shape, [[(0, 2, 3 - mine, 0)] for mine in range(2)], filled, weight=12000)
    filled = assemble((x, v, w), shape, [
        [(0, 0, 4 + mine, 0), (0, 1, 4 + mine, SIZES[2]), (1, 2, -1 - mine, 0), (1, 3, -1 - mine, SIZES[3])] + inner
        for mine, inner in enumerate(([], [(2, 0, -3, 0), (2, 1, -3, 1)]))], filled)
    return tuple(assemble((rest,), shape, [[(0, 3, 3 - mine, 0)] for mine in range(2)], filled))


def solution(mesh):
    return jax.shard_map(
        local,
        mesh=mesh,
        in_specs=(P(("grp", "chan"), None, None, None), P("grp", None), P("grp")),
        out_specs=(P(("grp", "chan"), None, None, None), P(("grp", "chan"), None, None, None)),
        check_vma=False,
    )
```

```python
import functools
import math

import jax
import jax.numpy as jnp
import numpy as np
from jax import lax
from jax.experimental import pallas as pl
from jax.experimental.pallas import tpu as pltpu
from jax.sharding import PartitionSpec as P

MAXP = 5
PLANE = 4
MIB = 1024 * 1024
ROWS = 16
STEP = 8

NEAR = (((0, 1), (0, 2), (1, 2)), ((0, 1), (0, 3), (1, 3)))
REST = (((0, 3), (1, 3), (2, 3)), ((0, 2), (1, 2), (2, 3)))
FIRST = ((-3, 2),)
BEYOND = ((0, 4), (0, 5), (1, 4), (1, 5), (3, 5))
OUTER = ((-1, 0), (-1, 2), (-1, 3), (-1, 4))
INNER = ((-2, 0), (-2, 1), (-2, 2), (-2, 3))
PAIRS = NEAR[0] + REST[0] + FIRST + BEYOND + OUTER + INNER
DESTS = ((0, 1), (2, 3), (4, 5), (-2, -1), (None, -3))


def flat(groups):
    return [pair for group in groups for pair in group]


def items(spot):
    ahead = sorted(("ahead", b - a - 1) for a, b in PAIRS if a == spot)
    back = sorted(("back", b - a - 1) for a, b in PAIRS if b == spot)
    return ahead + back


MERGED = (2, 3, 4)
SIZES = [max(len(items(spot)) for spot in spots) for spots in DESTS]
STARTS = [sum(SIZES[:d]) for d in range(len(SIZES))]
PLACE = {spot: (d, i) for d, spots in enumerate(DESTS) for i, spot in enumerate(spots)}


def lag_tables(lags):
    bins = lags // 2
    phase = (np.arange(lags)[:, None] * np.arange(1, bins + 1)[None, :] % lags) * (2.0 * math.pi / lags)
    real, imag = np.cos(phase), -np.sin(phase)
    causal = np.concatenate([real, imag], axis=1)
    other = np.concatenate([real, -imag], axis=1)
    near = np.concatenate([causal[:bins], causal[bins:][::-1]], axis=0)
    far = np.concatenate([other[bins:][::-1], other[:bins]], axis=0)
    return causal.astype(jnp.bfloat16), np.stack([near, far]).astype(jnp.bfloat16)


def whereabouts():
    me = lax.axis_index("chan").astype(jnp.int32)
    q = lax.rem(me, PLANE)
    far = q // 2
    return far, lax.rem(q, 2) ^ far, me - q, q


def whiten_body(mask_ref, table_ref, traces_ref, *refs):
    outs, (white, sems) = refs[:-2], refs[-2:]
    _, _, base, q = whereabouts()
    windows = white.shape[1]
    bins = table_ref.shape[0] // 2
    part = white.shape[-1]
    step = traces_ref.shape[1]
    at = pl.program_id(0)
    for n in range(step):
        w = at * step + n
        raw = jnp.dot(table_ref[...], traces_ref[0, n], preferred_element_type=jnp.float32)
        power = jnp.sum(raw * raw, axis=0, keepdims=True) / bins
        valid = mask_ref[base + q, w].astype(jnp.float32)
        scaled = (raw * (valid * lax.rsqrt(power + 1e-06))).astype(jnp.bfloat16)
        for quarter in range(2):
            piece = scaled[:, quarter * part:(quarter + 1) * part]
            white[quarter ^ lax.rem(q, 2), w, 0] = piece[:bins]
            white[quarter ^ lax.rem(q, 2), w, 1] = piece[bins:]

    def copies(i):
        span = pl.ds(i * step, step)
        targets = [(n, out.at[span]) for n, out in enumerate(outs)]
        if outs[0].shape[0] > windows:
            targets.append((1, outs[0].at[pl.ds(windows + i * step, step)]))
        return [pltpu.make_async_copy(white.at[k, span], target, sems.at[n, i]) for n, (k, target) in enumerate(targets)]

    for one in copies(at):
        one.start()

    @pl.when(at == pl.num_programs(0) - 1)
    def _():
        for i in range(sems.shape[1]):
            for one in copies(i):
                one.wait()


def whiten(mask, table, traces, lengths):
    _, windows, lags, width = traces.shape
    bins = lags // 2
    part = width // PLANE
    other = lengths[0] == windows

    def half(i):
        far = whereabouts()[0]
        return 0, i, 0, 1 - far if other else far

    return pl.pallas_call(
        whiten_body,
        grid=(windows // STEP,),
        in_specs=[
            pl.BlockSpec(memory_space=pltpu.SMEM),
            pl.BlockSpec((lags, lags), lambda i: (0, 0)),
            pl.BlockSpec((1, STEP, lags, 2 * part), half),
        ],
        out_specs=[pl.BlockSpec(memory_space=pl.ANY)] * len(lengths),
        out_shape=[jax.ShapeDtypeStruct((n, 2, bins, part), jnp.bfloat16) for n in lengths],
        scratch_shapes=[
            pltpu.VMEM((2, windows, 2, bins, part), jnp.bfloat16),
            pltpu.SemaphoreType.DMA((3, windows // STEP)),
        ],
        compiler_params=pltpu.CompilerParams(vmem_limit_bytes=57 * MIB),
        cost_estimate=pl.CostEstimate(flops=windows * lags * lags * width, bytes_accessed=2 * windows * lags * width, transcendentals=0),
    )(mask, table, traces)


def relayed(windows):
    return windows * 11 // 16


def correlate_body(counts_ref, table_ref, *refs, work, sources, filled):
    count = len(DESTS) + 1
    outs, stack = refs[-count - 1:-1], refs[-1]
    held, ins = refs[len(refs) - count - 1 - filled:-count - 1], refs[:len(refs) - count - 1 - filled]
    windows, _, bins, part = ins[1].shape
    far, m, base, _ = whereabouts()
    blocks = counts_ref.shape[0]
    scale = 1.0 / math.sqrt(windows)
    norm = 1.0 / math.sqrt(bins)

    def sum_up(group, at, where):
        need = sorted({spot for pair in group for spot in pair})
        edges = sorted({edge for s in need for _, start, stop in where[s] for edge in (start, stop)})

        def tile(kt, carry):
            top = pl.multiple_of(kt * ROWS, ROWS)
            rows = pl.ds(top, ROWS)
            sums = (jnp.zeros((ROWS, part), jnp.float32),) * (2 * len(group))
            for start, stop in zip(edges, edges[1:]):
                def window(w, sums, start=start):
                    real, imag = {}, {}
                    for s in need:
                        array, begin = [(a, start - first) for a, first, last in where[s] if first <= start < last][0]
                        real[s] = ins[array][begin + w, 0, rows, :].astype(jnp.float32)
                        imag[s] = ins[array][begin + w, 1, rows, :].astype(jnp.float32)
                    out = []
                    for n, (a, b) in enumerate(group):
                        out.append(sums[2 * n] + (real[a] * real[b] + imag[a] * imag[b]))
                        out.append(sums[2 * n + 1] + (imag[a] * real[b] - real[a] * imag[b]))
                    return tuple(out)

                sums = lax.fori_loop(0, stop - start, window, sums, unroll=stop - start if stop - start <= 12 else 8)
            for n in range(len(group)):
                lanes = pl.ds((at + n) * part, part)
                stack[rows, lanes] = (sums[2 * n] * scale).astype(jnp.bfloat16)
                stack[pl.ds(pl.multiple_of(bins + top, ROWS), ROWS), lanes] = (sums[2 * n + 1] * scale).astype(jnp.bfloat16)
            return carry

        lax.fori_loop(0, bins // ROWS, tile, 0)

    for mine in range(2):
        @pl.when(m == mine)
        def _(mine=mine):
            for out, old in zip(outs, held):
                out[...] = old[...]
            for g, group in enumerate(work[mine]):
                at = len(flat(work[mine][:g]))
                sum_up(group, at, sources[mine])
                lags = jnp.dot(table_ref[far], stack[:, at * part:(at + len(group)) * part], preferred_element_type=jnp.float32)
                for n, (a, b) in enumerate(group):
                    first = jnp.where(far == 0, base + a, base + 3 - b)
                    reach = counts_ref[jnp.clip(first, 0, blocks - 1)]
                    corr = lags[:, n * part:(n + 1) * part] * jnp.where(reach >= b - a, norm, 0.0)
                    for spot, kind, rows in ((a, "ahead", corr[:bins]), (b, "back", corr[bins:])):
                        d, i = PLACE[spot]
                        row = items(spot).index((kind, b - a - 1))
                        out, row = (outs[d], row) if i == mine else (outs[-1], STARTS[d] + row)
                        out[row] = rows.astype(jnp.bfloat16)


def correlate(counts, tables, whites, work, sources, filled=(), weight=1):
    windows, _, bins, part = whites[1].shape
    most = max(len(flat(groups)) for groups in work)
    scalars = pl.BlockSpec(memory_space=pltpu.SMEM)
    lengths = [size * (2 if d in MERGED else 1) for d, size in enumerate(SIZES)] + [sum(SIZES)]
    return pl.pallas_call(
        functools.partial(correlate_body, work=work, sources=sources, filled=len(filled)),
        in_specs=[scalars] + [pl.BlockSpec(memory_space=pltpu.VMEM)] * (1 + len(whites) + len(filled)),
        out_specs=[pl.BlockSpec(memory_space=pltpu.VMEM)] * len(lengths),
        out_shape=[jax.ShapeDtypeStruct((n, bins, part), jnp.bfloat16) for n in lengths],
        scratch_shapes=[pltpu.VMEM((2 * bins, most * part), jnp.bfloat16)],
        compiler_params=pltpu.CompilerParams(vmem_limit_bytes=12 * MIB),
        cost_estimate=pl.CostEstimate(flops=weight * 100 * most * windows * bins * part, bytes_accessed=min(weight, 1) * 4 * len(whites) * windows * bins * part, transcendentals=0),
    )(counts, tables, *whites, *filled)


def merge_body(sib, *refs):
    outs, sems = refs[len(MERGED):-1], refs[-1]
    copies = []
    for n, d in enumerate(MERGED):
        copies.append(pltpu.make_async_copy(
            sib.at[pl.ds(STARTS[d] - SIZES[0], SIZES[d])], outs[n].at[pl.ds(SIZES[d], SIZES[d])], sems.at[n]))
    for one in copies:
        one.start()
    for one in copies:
        one.wait()


def merge(sib, own):
    anywhere = pl.BlockSpec(memory_space=pl.ANY)
    return pl.pallas_call(
        merge_body,
        in_specs=[pl.BlockSpec(memory_space=pltpu.VMEM)] + [anywhere] * len(own),
        out_specs=[anywhere] * len(own),
        out_shape=[jax.ShapeDtypeStruct(value.shape, value.dtype) for value in own],
        scratch_shapes=[pltpu.SemaphoreType.DMA((len(own),))],
        input_output_aliases={1 + i: i for i in range(len(own))},
        compiler_params=pltpu.CompilerParams(vmem_limit_bytes=4 * MIB),
    )(sib, *own)


def assemble_body(*refs, plan, count, filled):
    ins, refs = refs[:count], refs[count + 2 * filled:]
    forward, backward, wide, sems = refs
    far, m, _, q = whereabouts()
    part = ins[0].shape[2]
    for mine in range(2):
        @pl.when(m == mine)
        def _(mine=mine):
            waits = []
            for a, k, spot, first in plan[mine]:
                lanes = pl.ds(pl.multiple_of((q ^ k) * part, part), part)
                ahead = far if k < 2 else 1 - far
                for n, (kind, j) in enumerate(items(spot)):
                    at = len(waits)
                    wide[at] = ins[a][first + n].astype(jnp.float32)
                    side = ahead if kind == "ahead" else 1 - ahead
                    copies = [pltpu.make_async_copy(wide.at[at], ref.at[0, j, :, lanes], sems.at[at]) for ref in (forward, backward)]
                    for value, copy in enumerate(copies):
                        pl.when(side == value)(copy.start)
                    waits.append(copies[0])
            for copy in waits:
                copy.wait()


def assemble(parts, shape, plan, filled=(), weight=1):
    steps = max(sum(len(items(spot)) for _, _, spot, _ in one) for one in plan)
    anywhere = pl.BlockSpec(memory_space=pl.ANY)
    bins, part = parts[0].shape[1:]
    return pl.pallas_call(
        functools.partial(assemble_body, plan=plan, count=len(parts), filled=len(filled) // 2),
        in_specs=[pl.BlockSpec(memory_space=pltpu.VMEM)] * len(parts) + [anywhere] * len(filled),
        out_specs=[anywhere] * 2,
        out_shape=[jax.ShapeDtypeStruct((1,) + shape, jnp.float32)] * 2,
        scratch_shapes=[pltpu.VMEM((steps, bins, part), jnp.float32), pltpu.SemaphoreType.DMA((steps,))],
        input_output_aliases={len(parts) + i: i for i in range(len(filled))},
        compiler_params=pltpu.CompilerParams(vmem_limit_bytes=12 * MIB),
        cost_estimate=pl.CostEstimate(flops=weight * steps * bins * part, bytes_accessed=6 * steps * bins * part, transcendentals=0),
    )(*parts, *filled)


HERE = (0, 0, 0, 0)
OUTWARD = (-1, -1, 1, 1)
INWARD = (1, 1, -1, -1)
INNER_HERE = (None, 0, 0, None)
INNER_INWARD = (None, 1, -1, None)
INNER_OUTWARD = (None, -1, 1, None)


def send(value, flip, step):
    peers = lax.axis_size("chan")
    pairs = []
    for i in range(peers):
        planes = step[i % PLANE]
        if planes is not None and 0 <= i + PLANE * planes < peers:
            pairs.append((i, (i ^ flip) + PLANE * planes))
    return lax.ppermute(value, "chan", pairs)


def after(value, *done):
    return lax.optimization_barrier((value,) + done)[0]


def local(traces, mask, counts):
    _, windows, lags, width = traces.shape
    causal, tables = lag_tables(lags)
    tables = jnp.asarray(tables)
    rows = jnp.asarray(np.ascontiguousarray(causal.T))
    t2, t3 = whiten(mask, rows, traces, (windows, windows))
    t01, t1 = whiten(after(mask, t2), rows, traces, (2 * windows, windows))

    y2, y3 = send(t2, 2, HERE), send(t3, 3, HERE)
    z, e = send(t01, 0, OUTWARD), send(t01, 0, INNER_INWARD)
    u1 = send(t1, 1, HERE)
    r2 = send(after(y2, u1), 0, INWARD)
    r3b = send(after(t3, y2)[relayed(windows):], 3, OUTWARD)

    whole = lambda *arrays: {spot: ((array, 0, windows),) for spot, array in arrays}
    parts = correlate(
        counts, tables, (t01, u1, y2), ((NEAR[0],), (NEAR[1],)), sources=(
            whole((0, 0), (1, 1), (2, 2)),
            whole((0, 1), (1, 0), (3, 2))), weight=200)
    r3a = send(after(y3, parts[4])[:relayed(windows)], 0, INWARD)
    e1 = send(after(e, parts[4])[windows:], 1, INNER_HERE)
    parts = correlate(
        counts, tables, (t01, u1, y2, y3), ((REST[0],), (REST[1],)), sources=(
            whole((0, 0), (1, 1), (2, 2), (3, 3)),
            whole((0, 1), (1, 0), (2, 3), (3, 2))), filled=parts, weight=200)
    half = windows // 2
    z = after(z, parts[4])
    z1a, z1b = send(z[windows:windows + half], 1, HERE), send(z[windows + half:], 1, HERE)
    other = ((5, 0, half), (6, half, windows))
    parts = correlate(
        counts, tables, (t01, u1, y2, y3, z, z1a, z1b, r2, e1, e), ((BEYOND, INNER, FIRST), (BEYOND, OUTER, FIRST)), sources=(
            whole((0, 0), (1, 1), (2, 2), (3, 3), (4, 4), (-2, 7), (-3, 8)) | {5: other},
            whole((0, 1), (1, 0), (2, 3), (3, 2), (5, 4), (-1, 7), (-3, 9)) | {4: other}), filled=parts, weight=0)
    last = ((5, 0, relayed(windows)), (6, relayed(windows), windows))
    keep, f, x, v, w, sib = correlate(
        counts, tables, (t01, u1, y2, y3, z, r3a, r3b), ((OUTER,), (INNER,)), sources=(
            whole((0, 0), (1, 1), (2, 2), (3, 3), (4, 4)) | {-1: last},
            whole((0, 1), (1, 0), (2, 3), (3, 2)) | {-2: last}), filled=parts)

    near = send(f, 2, HERE)
    others = send(sib[SIZES[0]:], 1, HERE)
    x, v, w = merge(others, (x, v, w))
    rest = send(others[:SIZES[1]], 2, HERE)
    twin = send(sib[:SIZES[0]], 1, HERE)
    v, x = send(v, 2, OUTWARD), send(x, 0, INWARD)
    w = send(w, 0, INNER_OUTWARD)

    shape = (MAXP, lags // 2, width)
    filled = assemble((keep, twin), shape, [[(0, 0, mine, 0), (1, 1, mine, 0)] for mine in range(2)])
    filled = assemble((near,), shape, [[(0, 2, 3 - mine, 0)] for mine in range(2)], filled, weight=12000)
    filled = assemble((x, v, w), shape, [
        [(0, 0, 4 + mine, 0), (0, 1, 4 + mine, SIZES[2]), (1, 2, -1 - mine, 0), (1, 3, -1 - mine, SIZES[3])] + inner
        for mine, inner in enumerate(([], [(2, 0, -3, 0), (2, 1, -3, 1)]))], filled)
    return tuple(assemble((rest,), shape, [[(0, 3, 3 - mine, 0)] for mine in range(2)], filled))


def solution(mesh):
    return jax.shard_map(
        local,
        mesh=mesh,
        in_specs=(P(("grp", "chan"), None, None, None), P("grp", None), P("grp")),
        out_specs=(P(("grp", "chan"), None, None, None), P(("grp", "chan"), None, None, None)),
        check_vma=False,
    )
```

```python
import functools
import math

import jax
import jax.numpy as jnp
import numpy as np
from jax import lax
from jax.experimental import pallas as pl
from jax.experimental.pallas import tpu as pltpu
from jax.sharding import PartitionSpec as P

MAXP = 5
PLANE = 4
MIB = 1024 * 1024
ROWS = 16
STEP = 8

NEAR = (((0, 1), (0, 2), (1, 2)), ((0, 1), (0, 3), (1, 3)))
REST = (((0, 3), (1, 3), (2, 3)), ((0, 2), (1, 2), (2, 3)))
FIRST = ((-3, 2),)
BEYOND = ((0, 4), (0, 5), (1, 4), (1, 5), (3, 5))
OUTER = ((-1, 0), (-1, 2), (-1, 3), (-1, 4))
INNER = ((-2, 0), (-2, 1), (-2, 2), (-2, 3))
PAIRS = NEAR[0] + REST[0] + FIRST + BEYOND + OUTER + INNER
DESTS = ((0, 1), (2, 3), (4, 5), (-2, -1), (None, -3))


def flat(groups):
    return [pair for group in groups for pair in group]


def items(spot):
    ahead = sorted(("ahead", b - a - 1) for a, b in PAIRS if a == spot)
    back = sorted(("back", b - a - 1) for a, b in PAIRS if b == spot)
    return ahead + back


MERGED = (2, 3, 4)
SIZES = [max(len(items(spot)) for spot in spots) for spots in DESTS]
STARTS = [sum(SIZES[:d]) for d in range(len(SIZES))]
PLACE = {spot: (d, i) for d, spots in enumerate(DESTS) for i, spot in enumerate(spots)}


def lag_tables(lags):
    bins = lags // 2
    phase = (np.arange(lags)[:, None] * np.arange(1, bins + 1)[None, :] % lags) * (2.0 * math.pi / lags)
    real, imag = np.cos(phase), -np.sin(phase)
    causal = np.concatenate([real, imag], axis=1)
    other = np.concatenate([real, -imag], axis=1)
    near = np.concatenate([causal[:bins], causal[bins:][::-1]], axis=0)
    far = np.concatenate([other[bins:][::-1], other[:bins]], axis=0)
    return causal.astype(jnp.bfloat16), np.stack([near, far]).astype(jnp.bfloat16)


def whereabouts():
    me = lax.axis_index("chan").astype(jnp.int32)
    q = lax.rem(me, PLANE)
    far = q // 2
    return far, lax.rem(q, 2) ^ far, me - q, q


def whiten_body(mask_ref, table_ref, traces_ref, *refs):
    outs, (white, sems) = refs[:-2], refs[-2:]
    _, _, base, q = whereabouts()
    windows = white.shape[1]
    bins = table_ref.shape[0] // 2
    part = white.shape[-1]
    step = traces_ref.shape[1]
    at = pl.program_id(0)
    for n in range(step):
        w = at * step + n
        raw = jnp.dot(table_ref[...], traces_ref[0, n], preferred_element_type=jnp.float32)
        power = jnp.sum(raw * raw, axis=0, keepdims=True) / bins
        valid = mask_ref[base + q, w].astype(jnp.float32)
        scaled = (raw * (valid * lax.rsqrt(power + 1e-06))).astype(jnp.bfloat16)
        for quarter in range(2):
            piece = scaled[:, quarter * part:(quarter + 1) * part]
            white[quarter ^ lax.rem(q, 2), w, 0] = piece[:bins]
            white[quarter ^ lax.rem(q, 2), w, 1] = piece[bins:]

    def copies(i):
        span = pl.ds(i * step, step)
        targets = [(n, out.at[span]) for n, out in enumerate(outs)]
        if outs[0].shape[0] > windows:
            targets.append((1, outs[0].at[pl.ds(windows + i * step, step)]))
        return [pltpu.make_async_copy(white.at[k, span], target, sems.at[n, i]) for n, (k, target) in enumerate(targets)]

    for one in copies(at):
        one.start()

    @pl.when(at == pl.num_programs(0) - 1)
    def _():
        for i in range(sems.shape[1]):
            for one in copies(i):
                one.wait()


def whiten(mask, table, traces, lengths):
    _, windows, lags, width = traces.shape
    bins = lags // 2
    part = width // PLANE
    other = lengths[0] == windows

    def half(i):
        far = whereabouts()[0]
        return 0, i, 0, 1 - far if other else far

    return pl.pallas_call(
        whiten_body,
        grid=(windows // STEP,),
        in_specs=[
            pl.BlockSpec(memory_space=pltpu.SMEM),
            pl.BlockSpec((lags, lags), lambda i: (0, 0)),
            pl.BlockSpec((1, STEP, lags, 2 * part), half),
        ],
        out_specs=[pl.BlockSpec(memory_space=pl.ANY)] * len(lengths),
        out_shape=[jax.ShapeDtypeStruct((n, 2, bins, part), jnp.bfloat16) for n in lengths],
        scratch_shapes=[
            pltpu.VMEM((2, windows, 2, bins, part), jnp.bfloat16),
            pltpu.SemaphoreType.DMA((3, windows // STEP)),
        ],
        compiler_params=pltpu.CompilerParams(vmem_limit_bytes=57 * MIB),
        cost_estimate=pl.CostEstimate(flops=windows * lags * lags * width, bytes_accessed=2 * windows * lags * width, transcendentals=0),
    )(mask, table, traces)


def relayed(windows):
    return windows * 11 // 16


def correlate_body(counts_ref, table_ref, *refs, work, sources, filled):
    count = len(DESTS) + 1
    outs, stack = refs[-count - 1:-1], refs[-1]
    held, ins = refs[len(refs) - count - 1 - filled:-count - 1], refs[:len(refs) - count - 1 - filled]
    windows, _, bins, part = ins[1].shape
    far, m, base, _ = whereabouts()
    blocks = counts_ref.shape[0]
    scale = 1.0 / math.sqrt(windows)
    norm = 1.0 / math.sqrt(bins)

    def sum_up(group, at, where):
        need = sorted({spot for pair in group for spot in pair})
        edges = sorted({edge for s in need for _, start, stop in where[s] for edge in (start, stop)})

        def tile(kt, carry):
            top = pl.multiple_of(kt * ROWS, ROWS)
            rows = pl.ds(top, ROWS)
            sums = (jnp.zeros((ROWS, part), jnp.float32),) * (2 * len(group))
            for start, stop in zip(edges, edges[1:]):
                def window(w, sums, start=start):
                    real, imag = {}, {}
                    for s in need:
                        array, begin = [(a, start - first) for a, first, last in where[s] if first <= start < last][0]
                        real[s] = ins[array][begin + w, 0, rows, :].astype(jnp.float32)
                        imag[s] = ins[array][begin + w, 1, rows, :].astype(jnp.float32)
                    out = []
                    for n, (a, b) in enumerate(group):
                        out.append(sums[2 * n] + (real[a] * real[b] + imag[a] * imag[b]))
                        out.append(sums[2 * n + 1] + (imag[a] * real[b] - real[a] * imag[b]))
                    return tuple(out)

                sums = lax.fori_loop(0, stop - start, window, sums, unroll=stop - start if stop - start <= 12 else 8)
            for n in range(len(group)):
                lanes = pl.ds((at + n) * part, part)
                stack[rows, lanes] = (sums[2 * n] * scale).astype(jnp.bfloat16)
                stack[pl.ds(pl.multiple_of(bins + top, ROWS), ROWS), lanes] = (sums[2 * n + 1] * scale).astype(jnp.bfloat16)
            return carry

        lax.fori_loop(0, bins // ROWS, tile, 0)

    for mine in range(2):
        @pl.when(m == mine)
        def _(mine=mine):
            for out, old in zip(outs, held):
                out[...] = old[...]
            for g, group in enumerate(work[mine]):
                at = len(flat(work[mine][:g]))
                sum_up(group, at, sources[mine])
                lags = jnp.dot(table_ref[far], stack[:, at * part:(at + len(group)) * part], preferred_element_type=jnp.float32)
                for n, (a, b) in enumerate(group):
                    first = jnp.where(far == 0, base + a, base + 3 - b)
                    reach = counts_ref[jnp.clip(first, 0, blocks - 1)]
                    corr = lags[:, n * part:(n + 1) * part] * jnp.where(reach >= b - a, norm, 0.0)
                    for spot, kind, rows in ((a, "ahead", corr[:bins]), (b, "back", corr[bins:])):
                        d, i = PLACE[spot]
                        row = items(spot).index((kind, b - a - 1))
                        out, row = (outs[d], row) if i == mine else (outs[-1], STARTS[d] + row)
                        out[row] = rows.astype(jnp.bfloat16)


def correlate(counts, tables, whites, work, sources, filled=(), weight=1):
    windows, _, bins, part = whites[1].shape
    most = max(len(flat(groups)) for groups in work)
    scalars = pl.BlockSpec(memory_space=pltpu.SMEM)
    lengths = [size * (2 if d in MERGED else 1) for d, size in enumerate(SIZES)] + [sum(SIZES)]
    return pl.pallas_call(
        functools.partial(correlate_body, work=work, sources=sources, filled=len(filled)),
        in_specs=[scalars] + [pl.BlockSpec(memory_space=pltpu.VMEM)] * (1 + len(whites) + len(filled)),
        out_specs=[pl.BlockSpec(memory_space=pltpu.VMEM)] * len(lengths),
        out_shape=[jax.ShapeDtypeStruct((n, bins, part), jnp.bfloat16) for n in lengths],
        scratch_shapes=[pltpu.VMEM((2 * bins, most * part), jnp.bfloat16)],
        compiler_params=pltpu.CompilerParams(vmem_limit_bytes=12 * MIB),
        cost_estimate=pl.CostEstimate(flops=weight * 100 * most * windows * bins * part, bytes_accessed=min(weight, 1) * 4 * len(whites) * windows * bins * part, transcendentals=0),
    )(counts, tables, *whites, *filled)


def merge_body(sib, *refs):
    outs, sems = refs[len(MERGED):-1], refs[-1]
    copies = []
    for n, d in enumerate(MERGED):
        copies.append(pltpu.make_async_copy(
            sib.at[pl.ds(STARTS[d] - SIZES[0], SIZES[d])], outs[n].at[pl.ds(SIZES[d], SIZES[d])], sems.at[n]))
    for one in copies:
        one.start()
    for one in copies:
        one.wait()


def merge(sib, own):
    anywhere = pl.BlockSpec(memory_space=pl.ANY)
    return pl.pallas_call(
        merge_body,
        in_specs=[pl.BlockSpec(memory_space=pltpu.VMEM)] + [anywhere] * len(own),
        out_specs=[anywhere] * len(own),
        out_shape=[jax.ShapeDtypeStruct(value.shape, value.dtype) for value in own],
        scratch_shapes=[pltpu.SemaphoreType.DMA((len(own),))],
        input_output_aliases={1 + i: i for i in range(len(own))},
        compiler_params=pltpu.CompilerParams(vmem_limit_bytes=4 * MIB),
    )(sib, *own)


def assemble_body(*refs, plan, count, filled):
    ins, refs = refs[:count], refs[count + 2 * filled:]
    forward, backward, wide, sems = refs
    far, m, _, q = whereabouts()
    part = ins[0].shape[2]
    for mine in range(2):
        @pl.when(m == mine)
        def _(mine=mine):
            waits = []
            for a, k, spot, first in plan[mine]:
                lanes = pl.ds(pl.multiple_of((q ^ k) * part, part), part)
                ahead = far if k < 2 else 1 - far
                for n, (kind, j) in enumerate(items(spot)):
                    at = len(waits)
                    wide[at] = ins[a][first + n].astype(jnp.float32)
                    side = ahead if kind == "ahead" else 1 - ahead
                    copies = [pltpu.make_async_copy(wide.at[at], ref.at[0, j, :, lanes], sems.at[at]) for ref in (forward, backward)]
                    for value, copy in enumerate(copies):
                        pl.when(side == value)(copy.start)
                    waits.append(copies[0])
            for copy in waits:
                copy.wait()


def assemble(parts, shape, plan, filled=(), weight=1):
    steps = max(sum(len(items(spot)) for _, _, spot, _ in one) for one in plan)
    anywhere = pl.BlockSpec(memory_space=pl.ANY)
    bins, part = parts[0].shape[1:]
    return pl.pallas_call(
        functools.partial(assemble_body, plan=plan, count=len(parts), filled=len(filled) // 2),
        in_specs=[pl.BlockSpec(memory_space=pltpu.VMEM)] * len(parts) + [anywhere] * len(filled),
        out_specs=[anywhere] * 2,
        out_shape=[jax.ShapeDtypeStruct((1,) + shape, jnp.float32)] * 2,
        scratch_shapes=[pltpu.VMEM((steps, bins, part), jnp.float32), pltpu.SemaphoreType.DMA((steps,))],
        input_output_aliases={len(parts) + i: i for i in range(len(filled))},
        compiler_params=pltpu.CompilerParams(vmem_limit_bytes=12 * MIB),
        cost_estimate=pl.CostEstimate(flops=weight * steps * bins * part, bytes_accessed=6 * steps * bins * part, transcendentals=0),
    )(*parts, *filled)


HERE = (0, 0, 0, 0)
OUTWARD = (-1, -1, 1, 1)
INWARD = (1, 1, -1, -1)
INNER_HERE = (None, 0, 0, None)
INNER_INWARD = (None, 1, -1, None)
INNER_OUTWARD = (None, -1, 1, None)


def send(value, flip, step):
    peers = lax.axis_size("chan")
    pairs = []
    for i in range(peers):
        planes = step[i % PLANE]
        if planes is not None and 0 <= i + PLANE * planes < peers:
            pairs.append((i, (i ^ flip) + PLANE * planes))
    return lax.ppermute(value, "chan", pairs)


def after(value, *done):
    return lax.optimization_barrier((value,) + done)[0]


def local(traces, mask, counts):
    _, windows, lags, width = traces.shape
    causal, tables = lag_tables(lags)
    tables = jnp.asarray(tables)
    rows = jnp.asarray(np.ascontiguousarray(causal.T))
    t2, t3 = whiten(mask, rows, traces, (windows, windows))
    t01, t1 = whiten(after(mask, t2), rows, traces, (2 * windows, windows))

    y2, y3 = send(t2, 2, HERE), send(t3, 3, HERE)
    z, e = send(t01, 0, OUTWARD), send(t01, 0, INNER_INWARD)
    u1 = send(t1, 1, HERE)
    r2 = send(after(y2, u1), 0, INWARD)
    r3b = send(after(t3, y2)[relayed(windows):], 3, OUTWARD)

    whole = lambda *arrays: {spot: ((array, 0, windows),) for spot, array in arrays}
    parts = correlate(
        counts, tables, (t01, u1, y2), ((NEAR[0],), (NEAR[1],)), sources=(
            whole((0, 0), (1, 1), (2, 2)),
            whole((0, 1), (1, 0), (3, 2))), weight=200)
    r3a = send(after(y3, parts[4])[:relayed(windows)], 0, INWARD)
    e1 = send(after(e, parts[4])[windows:], 1, INNER_HERE)
    parts = correlate(
        counts, tables, (t01, u1, y2, y3), ((REST[0],), (REST[1],)), sources=(
            whole((0, 0), (1, 1), (2, 2), (3, 3)),
            whole((0, 1), (1, 0), (2, 3), (3, 2))), filled=parts, weight=200)
    half = windows // 2
    z = after(z, parts[4])
    z1a, z1b = send(z[windows:windows + half], 1, HERE), send(z[windows + half:], 1, HERE)
    other = ((5, 0, half), (6, half, windows))
    parts = correlate(
        counts, tables, (t01, u1, y2, y3, z, z1a, z1b, r2, e1, e), ((BEYOND, INNER + FIRST), (BEYOND, OUTER + FIRST)), sources=(
            whole((0, 0), (1, 1), (2, 2), (3, 3), (4, 4), (-2, 7), (-3, 8)) | {5: other},
            whole((0, 1), (1, 0), (2, 3), (3, 2), (5, 4), (-1, 7), (-3, 9)) | {4: other}), filled=parts, weight=0)
    last = ((5, 0, relayed(windows)), (6, relayed(windows), windows))
    keep, f, x, v, w, sib = correlate(
        counts, tables, (t01, u1, y2, y3, z, r3a, r3b), ((OUTER,), (INNER,)), sources=(
            whole((0, 0), (1, 1), (2, 2), (3, 3), (4, 4)) | {-1: last},
            whole((0, 1), (1, 0), (2, 3), (3, 2)) | {-2: last}), filled=parts)

    near = send(f, 2, HERE)
    others = send(sib[SIZES[0]:], 1, HERE)
    x, v, w = merge(others, (x, v, w))
    rest = send(others[:SIZES[1]], 2, HERE)
    twin = send(sib[:SIZES[0]], 1, HERE)
    v, x = send(v, 2, OUTWARD), send(x, 0, INWARD)
    w = send(w, 0, INNER_OUTWARD)

    shape = (MAXP, lags // 2, width)
    filled = assemble((keep, twin), shape, [[(0, 0, mine, 0), (1, 1, mine, 0)] for mine in range(2)])
    filled = assemble((near,), shape, [[(0, 2, 3 - mine, 0)] for mine in range(2)], filled, weight=12000)
    filled = assemble((x, v, w), shape, [
        [(0, 0, 4 + mine, 0), (0, 1, 4 + mine, SIZES[2]), (1, 2, -1 - mine, 0), (1, 3, -1 - mine, SIZES[3])] + inner
        for mine, inner in enumerate(([], [(2, 0, -3, 0), (2, 1, -3, 1)]))], filled)
    return tuple(assemble((rest,), shape, [[(0, 3, 3 - mine, 0)] for mine in range(2)], filled))


def solution(mesh):
    return jax.shard_map(
        local,
        mesh=mesh,
        in_specs=(P(("grp", "chan"), None, None, None), P("grp", None), P("grp")),
        out_specs=(P(("grp", "chan"), None, None, None), P(("grp", "chan"), None, None, None)),
        check_vma=False,
    )
```
